256 devices in a mesh: pair: 8 (over x, core), mesh: 32 (over y, z).
Axes of the slice: x: 4, y: 4, z: 8, core: 2. Of those that a mesh axis runs over, the one named last changes fastest.
Arguments:
- psi: bfloat16 [8, 343, 8192], P(None, None, 'mesh'), may hold values from -6 to 6
- kappa: float32 [256, 32, 128], P('mesh'), may hold values from 0.1 to 6
- interp_down: bfloat16 [128, 343], replicated, may hold values from -0.3125 to 0.3125
- interp_up: bfloat16 [343, 128], replicated, may hold values from -0.5 to 0.5
- brick_of_cell: int32 [8192], P('mesh'), may hold values from 0 to 8191, as said below
- pair_first: int32 [32], P('pair'), may hold values from 0 to 7
- pair_second: int32 [32], P('pair'), may hold values from 0 to 7
Outputs:
- potential: float32 [32, 256, 32, 128], P('pair', 'mesh')
- action: float32 [8, 343, 8192], P('pair', None, 'mesh')
The draws below stay inside these ranges and needn't reach their ends.
Inputs may be any that keep to these rules, and one draw needn't show every extreme that they name: `brick_of_cell`: A permutation of the bricks. The cells of one partition go to partitions at most 16 to any one partition, exactly 16 to its own; how many partition m sends to partition (m + k) mod 32 depends on k only.
All inputs are finite; a program needn't handle non-finite values.
Results may differ from the reference program's by a relative error of at most 0.0008.
The reference program's roundings to bfloat16 on the way (of `dens`, `rho` and `cellv`) count: a program that leaves them out, or rounds other values in their place, can miss the bound.
Values may be sent and summed in bfloat16 or wider, within the bound.
No kernel may reach another device: no remote copies, remote signals or barrier semaphores. Data moves between devices by JAX's collectives and lax.ppermute only.
A program may use at most 64 MiB of HBM per device.

```python
import math
import jax
import jax.numpy as jnp
from jax import lax

NODES_W = 343
NODES_E = 128
ORB = 8
PAIRS = 32
ITERS = 2
GZ = 8
GY = 32
GX = 128
CW = 256
CELLS = 8192
NZ = 256
N_MESH = 32


def draw_brick_of_cell(key, part):
    key = jax.random.fold_in(key, 11)
    lanes = N_MESH
    share = CW // N_MESH
    first, second, third = jax.random.split(key, 3)
    offsets = jnp.arange(lanes, dtype=jnp.int32)
    partner = (lanes - offsets) % lanes
    deltas = jax.random.randint(first, (lanes,), -share, share + 1, dtype=jnp.int32)
    counts = jnp.where(offsets < partner, share + deltas, share - deltas[partner])
    counts = jnp.where(offsets == lanes // 2, share, counts)
    counts = jnp.where(offsets == 0, 2 * share, counts)
    near_one = (share + deltas[1]) // 2
    counts = jnp.where(offsets == 1, near_one, counts)
    counts = jnp.where(offsets == lanes - 1, share - near_one, counts)
    ends = jnp.cumsum(counts)
    places = jnp.arange(CW, dtype=jnp.int32)
    group = jnp.sum((places[:, None] >= ends[None, :]).astype(jnp.int32), axis=1)
    slots = jax.vmap(lambda k: jax.random.permutation(k, CW))(jax.random.split(second, lanes)).astype(jnp.int32)
    order = jax.vmap(lambda k: jax.random.permutation(k, CW))(jax.random.split(third, lanes)).astype(jnp.int32)
    sender = offsets[:, None]
    target = (sender + group[None, :]) % lanes
    value = target * CW + slots[target, places[None, :]]
    where_cell = (sender * CW + order).reshape(-1)
    return jnp.zeros((lanes * CW,), jnp.int32).at[where_cell].set(value.reshape(-1))


def set_ends(entries, own_key, low, high):
    dims = entries.shape
    place = [jax.random.randint(jax.random.fold_in(own_key, axis), (), 0, dims[axis]) for axis in range(len(dims))]
    entries = entries.at[tuple(place)].set(low)
    longest = dims.index(max(dims))
    place[longest] = (place[longest] + 1) % dims[longest]
    return entries.at[tuple(place)].set(high)


def block_scale(own_key, extent, shards, smallest, top_value):
    def one(axis_at, blocks):
        heights = jax.random.uniform(jax.random.fold_in(jax.random.fold_in(own_key, 6), axis_at), (blocks,), jnp.float32, smallest / len(shards), top_value / len(shards))
        return jnp.repeat(jnp.exp(heights), extent[axis_at] // blocks).reshape((-1,) + (1,) * (len(extent) - axis_at - 1))

    factor_of = one(*shards[0])
    for cut in shards[1:]:
        factor_of = factor_of * one(*cut)
    return factor_of


def centred(stream_key, dims, scale, limit, cuts=(), kind=jnp.bfloat16):
    drawn = scale * jax.random.normal(stream_key, dims, jnp.float32)
    if cuts:
        drawn = drawn * block_scale(stream_key, dims, cuts, -0.22, 0.18)
    return jnp.clip(drawn, -limit, limit).astype(kind)


def setup_inputs(seed: int = 0) -> dict:
    seeds = jax.random.split(jax.random.key(seed), 8)
    return {
        "psi": centred(seeds[0], (ORB, NODES_W, CELLS), 1.0, 6.0, ((2, 32),)),
        "kappa": jnp.clip(jnp.exp(math.log(6.0) - 4.0943445 * jax.random.uniform(seeds[1], (NZ, GY, GX), jnp.float32) ** block_scale(seeds[1], (NZ, GY, GX), ((0, 32),), -0.2, 0.2)), 0.1, 6.0),
        "interp_down": centred(seeds[2], (NODES_E, NODES_W), NODES_W ** -0.5, 0.3125),
        "interp_up": centred(seeds[3], (NODES_W, NODES_E), NODES_E ** -0.5, 0.5),
        "brick_of_cell": draw_brick_of_cell(jax.random.fold_in(seeds[7], 71), 0),
        "pair_first": set_ends(jax.random.randint(seeds[5], (PAIRS,), 0, ORB), jax.random.fold_in(seeds[5], 1), 0, ORB - 1).astype(jnp.int32),
        "pair_second": set_ends(jax.random.randint(seeds[6], (PAIRS,), 0, ORB), jax.random.fold_in(seeds[6], 1), 0, ORB - 1).astype(jnp.int32),
    }


four_pi = 4.0 * math.pi


def bricks_to_grid(bricks, depth, height, width):
    lead = bricks.shape[0]
    shaped = bricks.reshape(lead, 2, 4, 16, depth // 2, height // 4, width // 16)
    return shaped.transpose(0, 4, 1, 5, 2, 6, 3).reshape(lead, depth, height, width)


def grid_to_bricks(grid):
    lead, depth, height, width = grid.shape
    shaped = grid.reshape(lead, depth // 2, 2, height // 4, 4, width // 16, 16)
    return shaped.transpose(0, 2, 4, 6, 1, 3, 5).reshape(lead, 128, -1)


def beside(padded):
    center = padded[:, 1:-1]
    total = padded[:, 2:] + padded[:, :-2]
    wide_y = jnp.pad(center, ((0, 0), (0, 0), (1, 1), (0, 0)))
    total = total + wide_y[:, :, 2:] + wide_y[:, :, :-2]
    wide_x = jnp.pad(center, ((0, 0), (0, 0), (0, 0), (1, 1)))
    return total + wide_x[:, :, :, 2:] + wide_x[:, :, :, :-2]


def reference(psi, kappa, interp_down, interp_up, brick_of_cell, pair_first, pair_second):
    dens = (psi[pair_first].astype(jnp.float32) * psi[pair_second].astype(jnp.float32)).astype(jnp.bfloat16)
    rho = jnp.einsum("en,pnc->pec", interp_down.astype(jnp.float32), dens.astype(jnp.float32)).astype(jnp.bfloat16)
    placed = jnp.zeros((PAIRS, NODES_E, CELLS), jnp.bfloat16).at[:, :, brick_of_cell].set(rho)
    parts = placed.reshape(PAIRS, NODES_E, N_MESH, CW).transpose(0, 2, 1, 3).reshape(PAIRS * N_MESH, NODES_E, CW)
    grid = bricks_to_grid(parts, GZ, GY, GX).reshape(PAIRS, NZ, GY, GX)
    rhs = four_pi * grid.astype(jnp.float32)
    diag = 6.0 + kappa

    def apply(field):
        padded = jnp.pad(field, ((0, 0), (1, 1), (0, 0), (0, 0)))
        return diag * field - beside(padded)

    def dot(left, right):
        return jnp.sum(left * right, axis=(1, 2, 3))

    resid = rhs
    precond = resid / diag
    dirn = precond
    gamma = dot(resid, precond)
    solution = jnp.zeros_like(rhs)
    for step in range(ITERS):
        image = apply(dirn)
        alpha = gamma / dot(dirn, image)
        solution = solution + alpha[:, None, None, None] * dirn
        if step + 1 < ITERS:
            resid = resid - alpha[:, None, None, None] * image
            precond = resid / diag
            fresh = dot(resid, precond)
            dirn = precond + (fresh / gamma)[:, None, None, None] * dirn
            gamma = fresh
    rounded = solution.astype(jnp.bfloat16)
    back = grid_to_bricks(rounded.reshape(PAIRS * N_MESH, GZ, GY, GX))
    back = back.reshape(PAIRS, N_MESH, NODES_E, CW).transpose(0, 2, 1, 3).reshape(PAIRS, NODES_E, CELLS)
    cellv = back[:, :, brick_of_cell]
    upward = jnp.einsum("ne,pec->pnc", interp_up.astype(jnp.float32), cellv.astype(jnp.float32))
    term = upward * psi[pair_second].astype(jnp.float32)
    select = (pair_first[:, None] == jnp.arange(ORB, dtype=jnp.int32)[None, :]).astype(jnp.float32)
    action = jnp.einsum("po,pnc->onc", select, term, precision=lax.Precision.HIGHEST)
    return solution, action
```

```python
import math

import jax
import jax.numpy as jnp
from jax import lax
from jax.experimental import pallas as pl
from jax.experimental.pallas import tpu as pltpu
from jax.sharding import PartitionSpec as P

F32 = jnp.float32
BF16 = jnp.bfloat16
I32 = jnp.int32
FOUR_PI = 4.0 * math.pi

LANES = 32
BOUND = 16
CELLS = 256
SLOTS = LANES * BOUND
NODES_W = 343
NODES_E = 128
LOCAL = 4
ORB = 8
GZ, GY, GX = 8, 32, 128
WIDE = LOCAL * NODES_E
META = 16

VMEM = pl.BlockSpec(memory_space=pltpu.VMEM)
SMEM = pl.BlockSpec(memory_space=pltpu.SMEM)
PARAMS = pltpu.CompilerParams(vmem_limit_bytes=40 * 1024 * 1024)


def iota(shape, dim):
    return lax.broadcasted_iota(I32, shape, dim)


def onehot(condition):
    return jnp.where(condition, 1.0, 0.0).astype(BF16)


def dot(left, right):
    return lax.dot_general(left, right, (((1,), (0,)), ((), ())), preferred_element_type=F32)


def dot_nt(left, right):
    return lax.dot_general(left, right, (((1,), (1,)), ((), ())), preferred_element_type=F32)


def call(body, out, specs, args, scratch=(), flops=10**7):
    return pl.pallas_call(
        body,
        out_shape=out,
        in_specs=specs,
        out_specs=jax.tree.map(lambda _: VMEM, out),
        scratch_shapes=list(scratch),
        compiler_params=PARAMS,
        cost_estimate=pl.CostEstimate(flops=flops, bytes_accessed=2**21, transcendentals=0),
    )(*args)


def swap_groups(tiles):
    group = iota((8, 128), 1) >> 4
    for bit in (1, 2, 4):
        low = (group & bit) == 0
        mixed = list(tiles)
        for i in range(8):
            if i & bit == 0:
                j = i | bit
                mixed[i] = jnp.where(low, tiles[i], pltpu.roll(tiles[j], 16 * bit, 1))
                mixed[j] = jnp.where(low, pltpu.roll(tiles[i], 128 - 16 * bit, 1), tiles[j])
        tiles = mixed
    return tiles


def plane_of(kappa, z):
    return jnp.concatenate([kappa[z, pl.ds(c, 8, stride=4), :] for c in range(4)], axis=0)


def beside_xy(plane):
    row, lane = iota((8, 128), 0), iota((GY, 128), 1)
    first, last = plane[0:8], plane[24:32]
    above = jnp.where(row < 7, pltpu.roll(first, 7, 0), 0.0)
    below = jnp.where(row > 0, pltpu.roll(last, 1, 0), 0.0)
    along_y = jnp.concatenate([plane[8:32], above], axis=0) + jnp.concatenate(
        [below, plane[0:24]], axis=0
    )
    right = jnp.where(lane < 127, pltpu.roll(plane, 127, 1), 0.0)
    left = jnp.where(lane > 0, pltpu.roll(plane, 1, 1), 0.0)
    return along_y + right + left


def pack_kernel(first, second, row, col, down, psi, out, pick):
    target_row, target_col = row[...] >> 8, col[...] >> 8
    here, there = iota((CELLS, CELLS), 0), iota((CELLS, CELLS), 1)
    same = target_col == target_row
    rank_row = jnp.sum(jnp.where(same & (here < there), 1, 0), axis=0, keepdims=True)
    rank_col = jnp.sum(jnp.where(same & (there < here), 1, 0), axis=1, keepdims=True)
    position_row = target_row * BOUND + rank_row
    position_col = target_col * BOUND + rank_col
    sel = onehot(iota((SLOTS, CELLS), 0) == position_row)
    pick[...] = onehot(iota((CELLS, SLOTS), 1) == position_col)
    for p in range(LOCAL):
        left, right = psi[first[p]].astype(F32), psi[second[p]].astype(F32)
        rho = dot(down[...], (left * right).astype(BF16)).astype(BF16)
        out[:, p * NODES_E : (p + 1) * NODES_E] = dot_nt(sel, rho).astype(BF16)
    number = ((row[...] & 255) - CELLS).astype(F32).astype(BF16)
    number = dot_nt(sel, jnp.broadcast_to(number, (NODES_E, CELLS)))
    out[:, WIDE:] = (number + float(CELLS)).astype(BF16)


def place_kernel(arrived, kappa, u_out, up_out, down_out, number_out, placed):
    number_out[...] = arrived[:, WIDE:]
    probe = onehot(iota((8, 128), 1) == 0)
    number = dot_nt(probe, arrived[:, WIDE:])[0:1].astype(I32)
    sel = onehot(iota((CELLS, SLOTS), 0) == number)
    for p in range(LOCAL):
        placed[p] = dot(sel, arrived[:, p * 128 : (p + 1) * 128])
    diag = [6.0 + plane_of(kappa, z) for z in range(GZ)]
    for bz in range(4):
        for p in range(LOCAL):
            tiles = swap_groups(
                [placed[p, pl.ds(bz * 64 + bx, 8, stride=8), :] for bx in range(8)]
            )
            for a in range(2):
                z = 2 * bz + a
                u = FOUR_PI * jnp.concatenate(tiles[4 * a : 4 * a + 4], axis=0) / diag[z]
                u_out[p, z] = u
                if bz == 3:
                    up_out[(p * 2 + a) * GY : (p * 2 + a + 1) * GY] = u
                if z == 0:
                    down_out[p * GY : (p + 1) * GY] = u
    up_out[LOCAL * 2 * GY :] = plane_of(kappa, GZ - 1)


def krylov_kernel(inner, u_ref, up, down, kappa, w_out, sums_out):
    keep = inner[0].astype(F32)
    diag = [6.0 + up[LOCAL * 2 * GY :]] + [6.0 + plane_of(kappa, z) for z in range(GZ)]
    inverse = [1.0 / d for d in diag]
    rows = []
    for p in range(LOCAL):
        u = [up[(p * 2 + a) * GY : (p * 2 + a + 1) * GY] for a in range(2)]
        u += [u_ref[p, z] for z in range(GZ)] + [down[p * GY : (p + 1) * GY]]
        gamma = delta = eps = cross = jnp.zeros((GY, 128), F32)
        before = None
        for z in range(-1, GZ):
            centre = u[z + 2]
            scaled = diag[z + 1] * centre
            image = scaled - (u[z + 1] + u[z + 3] + beside_xy(centre))
            w = image * inverse[z + 1]
            if z < 0:
                before = w * keep
                continue
            w_out[p, z] = w
            gamma += scaled * centre
            delta += centre * image
            eps += image * w
            cross += w * (beside_xy(w) + 2.0 * before)
            before = w
        rows += [jnp.sum(v, axis=0, keepdims=True) for v in (gamma, delta, eps, eps - cross)]
    sums = jnp.sum(jnp.concatenate(rows, axis=0), axis=1, keepdims=True)
    spread = jnp.where(iota((16, 128), 1) == iota((16, 128), 0), sums, 0.0)
    sums_out[...] = jnp.broadcast_to(jnp.sum(spread, axis=0, keepdims=True), (LANES, 128))


def finish_kernel(sums, u_ref, w_ref, number, potential, out, bricks):
    total = jnp.sum(sums[...], axis=0, keepdims=True)
    lane = iota((1, 128), 1)
    for p in range(LOCAL):
        gamma, delta, eps, zeta = (
            jnp.sum(jnp.where(lane == 4 * p + k, total, 0.0), axis=1, keepdims=True) for k in range(4)
        )
        alpha = gamma / delta
        fresh = alpha * alpha * eps - gamma
        grow = 1.0 + fresh / gamma
        energy = grow * grow * delta - 2.0 * grow * alpha * eps + alpha * alpha * zeta
        later = fresh / energy
        on_u = jnp.broadcast_to(alpha + later * grow, (GY, 128))
        on_w = jnp.broadcast_to(later * alpha, (GY, 128))
        for bz in range(4):
            tiles = []
            for a in range(2):
                z = 2 * bz + a
                x = on_u * u_ref[p, z] - on_w * w_ref[p, z]
                for c in range(4):
                    tile = x[8 * c : 8 * c + 8]
                    potential[p, z, pl.ds(c, 8, stride=4), :] = tile
                    tiles.append(tile)
            for bx, tile in enumerate(swap_groups(tiles)):
                bricks[p, pl.ds(bz * 64 + bx, 8, stride=8), :] = tile
    wanted = number[...].astype(F32).astype(I32)
    lane = iota((SLOTS, 128), 1)
    sel = onehot(jnp.concatenate([wanted == lane, wanted == lane + 128], axis=1))
    for p in range(LOCAL):
        out[:, p * 128 : (p + 1) * 128] = dot(sel, bricks[p].astype(BF16)).astype(BF16)


def cells_kernel(first, second, pick, returned, head, tail):
    half = CELLS // 2
    cellv = dot(pick[...], returned[...]).astype(BF16)
    head[:half] = cellv[:half]
    tail[...] = cellv[half:]
    lane = iota((META, 128), 1)
    for p in range(LOCAL):
        orbitals = jnp.where(lane < 64, first[p], second[p]).astype(F32).astype(BF16)
        head[half:, p * 128 : (p + 1) * 128] = orbitals


def action_kernel(me, up, psi, *refs):
    blocks, (out, meta, scalars, sem) = refs[:-4], refs[-4:]
    half = CELLS // 2
    blocks = [(blocks[2 * i], blocks[2 * i + 1]) for i in range(ORB)]
    for i, (head, _) in enumerate(blocks):
        meta[8 * i : 8 * i + 8] = head[half:].astype(F32).astype(I32)[0:8]
    copy = pltpu.make_async_copy(meta, scalars, sem)
    copy.start()
    out[...] = jnp.zeros_like(out)
    copy.wait()
    for i, (head, tail) in enumerate(blocks):
        for p in range(LOCAL):

            @pl.when(scalars[8 * i, p * 128] == me[0])
            def _():
                orbital = psi[scalars[8 * i, p * 128 + 64]].astype(F32)
                cut = slice(p * 128, (p + 1) * 128)
                out[0, :, :half] += dot_nt(up[...], head[:half, cut]) * orbital[:, :half]
                out[0, :, half:] += dot_nt(up[...], tail[:, cut]) * orbital[:, half:]


def on_device(psi, kappa, interp_down, interp_up, brick_of_cell, pair_first, pair_second):
    struct = jax.ShapeDtypeStruct
    field = struct((LOCAL, GZ, GY, GX), F32)
    out, pick = call(
        pack_kernel,
        (struct((SLOTS, WIDE + 128), BF16), struct((CELLS, SLOTS), BF16)),
        [SMEM, SMEM, VMEM, VMEM, VMEM, VMEM],
        (
            pair_first,
            pair_second,
            brick_of_cell.reshape(1, CELLS),
            brick_of_cell.reshape(CELLS, 1),
            interp_down,
            psi,
        ),
    )
    arrived = lax.all_to_all(out, "mesh", 0, 0, tiled=True)
    u, up, down, number = call(
        place_kernel,
        (
            field,
            struct(((LOCAL * 2 + 1) * GY, GX), F32),
            struct((LOCAL * GY, GX), F32),
            struct((SLOTS, 128), BF16),
        ),
        [VMEM, VMEM],
        (arrived, kappa),
        [pltpu.VMEM((LOCAL, CELLS, NODES_E), F32)],
    )
    up = lax.ppermute(up, "mesh", [(i, i + 1) for i in range(LANES - 1)])
    down = lax.ppermute(down, "mesh", [(i + 1, i) for i in range(LANES - 1)])
    inner = (lax.axis_index("mesh") > 0).astype(I32).reshape(1)
    w, sums = call(
        krylov_kernel,
        (field, struct((LANES, 128), F32)),
        [SMEM, VMEM, VMEM, VMEM, VMEM],
        (inner, u, up, down, kappa),
    )
    sums = lax.all_to_all(sums, "mesh", 0, 0, tiled=True)
    potential, back = call(
        finish_kernel,
        (field, struct((SLOTS, WIDE), BF16)),
        [VMEM, VMEM, VMEM, VMEM],
        (sums, u, w, number),
        [pltpu.VMEM((LOCAL, CELLS, NODES_E), F32)],
    )
    returned = lax.all_to_all(back, "mesh", 0, 0, tiled=True)
    half = CELLS // 2
    head, tail = call(
        cells_kernel,
        (struct((half + META, WIDE), BF16), struct((half, WIDE), BF16)),
        [SMEM, SMEM, VMEM, VMEM],
        (pair_first, pair_second, pick, returned),
    )

    def shift(value, by):
        return lax.ppermute(value, "pair", [(i, (i + by) % ORB) for i in range(ORB)])

    def sibling(value):
        return lax.ppermute(value, "pair", [(i, i ^ 1) for i in range(ORB)])

    own = (head, tail)
    right = (shift(head, 2), shift(tail, 2))
    left = (shift(head, -2), shift(tail, -2))
    across = (shift(right[0], 2), shift(left[1], -2))
    blocks = []
    for pieces in (own, right, left, across):
        blocks += [*pieces, sibling(pieces[0]), sibling(pieces[1])]
    action = call(
        action_kernel,
        struct((1, NODES_W, CELLS), F32),
        [SMEM, VMEM, VMEM] + [VMEM] * len(blocks),
        (lax.axis_index("pair").astype(I32).reshape(1), interp_up, psi, *blocks),
        [pltpu.VMEM((8 * ORB, WIDE), I32), pltpu.SMEM((8 * ORB, WIDE), I32), pltpu.SemaphoreType.DMA],
    )
    return potential, action


def solution(mesh):
    return jax.shard_map(
        on_device,
        mesh=mesh,
        in_specs=(
            P(None, None, "mesh"),
            P("mesh", None, None),
            P(),
            P(),
            P("mesh"),
            P("pair"),
            P("pair"),
        ),
        out_specs=(P("pair", "mesh", None, None), P("pair", None, "mesh")),
        check_vma=False,
    )
```

```python
import functools
import math

import jax
import jax.numpy as jnp
from jax import lax
from jax.experimental import pallas as pl
from jax.experimental.pallas import tpu as pltpu
from jax.sharding import PartitionSpec as P

F32 = jnp.float32
BF16 = jnp.bfloat16
I32 = jnp.int32
FOUR_PI = 4.0 * math.pi

LANES = 32
BOUND = 16
CELLS = 256
SLOTS = LANES * BOUND
NODES_W = 343
NODES_E = 128
LOCAL = 4
ORB = 8
GZ, GY, GX = 8, 32, 128
WIDE = LOCAL * NODES_E
META = 16

VMEM = pl.BlockSpec(memory_space=pltpu.VMEM)
SMEM = pl.BlockSpec(memory_space=pltpu.SMEM)
PARAMS = pltpu.CompilerParams(vmem_limit_bytes=40 * 1024 * 1024)


def iota(shape, dim):
    return lax.broadcasted_iota(I32, shape, dim)


def onehot(condition):
    return jnp.where(condition, 1.0, 0.0).astype(BF16)


def dot(left, right):
    return lax.dot_general(left, right, (((1,), (0,)), ((), ())), preferred_element_type=F32)


def dot_nt(left, right):
    return lax.dot_general(left, right, (((1,), (1,)), ((), ())), preferred_element_type=F32)


def dot_tn(left, right):
    return lax.dot_general(left, right, (((0,), (0,)), ((), ())), preferred_element_type=F32)


def call(body, out, specs, args, scratch=(), flops=10**7):
    return pl.pallas_call(
        body,
        out_shape=out,
        in_specs=specs,
        out_specs=jax.tree.map(lambda _: VMEM, out),
        scratch_shapes=list(scratch),
        compiler_params=PARAMS,
        cost_estimate=pl.CostEstimate(flops=flops, bytes_accessed=2**21, transcendentals=0),
    )(*args)


def swap_groups(tiles):
    group = iota((8, 128), 1) >> 4
    for bit in (1, 2, 4):
        low = (group & bit) == 0
        mixed = list(tiles)
        for i in range(8):
            if i & bit == 0:
                j = i | bit
                mixed[i] = jnp.where(low, tiles[i], pltpu.roll(tiles[j], 16 * bit, 1))
                mixed[j] = jnp.where(low, pltpu.roll(tiles[i], 128 - 16 * bit, 1), tiles[j])
        tiles = mixed
    return tiles


def plane_of(kappa, z):
    return jnp.concatenate([kappa[z, pl.ds(c, 8, stride=4), :] for c in range(4)], axis=0)


def beside_xy(plane):
    row, lane = iota((8, 128), 0), iota((GY, 128), 1)
    first, last = plane[0:8], plane[24:32]
    above = jnp.where(row < 7, pltpu.roll(first, 7, 0), 0.0)
    below = jnp.where(row > 0, pltpu.roll(last, 1, 0), 0.0)
    along_y = jnp.concatenate([plane[8:32], above], axis=0) + jnp.concatenate(
        [below, plane[0:24]], axis=0
    )
    right = jnp.where(lane < 127, pltpu.roll(plane, 127, 1), 0.0)
    left = jnp.where(lane > 0, pltpu.roll(plane, 1, 1), 0.0)
    return along_y + right + left


def positions(row):
    target = row >> 8
    member = iota((LANES, CELLS), 0) == target
    order = onehot(iota((CELLS, CELLS), 0) < iota((CELLS, CELLS), 1))
    rank = jnp.where(member, dot(onehot(member), order), 0.0)
    return target * BOUND + jnp.sum(rank, axis=0, keepdims=True).astype(I32)


def pack_kernel(first, second, row, down, psi, out):
    sel = onehot(iota((SLOTS, CELLS), 0) == positions(row[...]))
    for p in range(LOCAL):
        left, right = psi[first[p]].astype(F32), psi[second[p]].astype(F32)
        rho = dot_tn(down[...], (left * right).astype(BF16)).astype(BF16)
        out[:, p * NODES_E : (p + 1) * NODES_E] = dot_nt(sel, rho).astype(BF16)
    number = ((row[...] & 255) - CELLS).astype(F32).astype(BF16)
    number = dot_nt(sel, jnp.broadcast_to(number, (NODES_E, CELLS)))
    out[:, WIDE:] = (number + float(CELLS)).astype(BF16)


def place_kernel(arrived, kappa, u_out, up_out, down_out, number_out, placed):
    number_out[...] = arrived[:, WIDE:]
    probe = onehot(iota((8, 128), 1) == 0)
    number = dot_nt(probe, arrived[:, WIDE:])[0:1].astype(I32)
    sel = onehot(iota((CELLS, SLOTS), 0) == number)
    for p in range(LOCAL):
        placed[p] = dot(sel, arrived[:, p * 128 : (p + 1) * 128])
    diag = [6.0 + plane_of(kappa, z) for z in range(GZ)]
    for bz in range(4):
        for p in range(LOCAL):
            tiles = swap_groups(
                [placed[p, pl.ds(bz * 64 + bx, 8, stride=8), :] for bx in range(8)]
            )
            for a in range(2):
                z = 2 * bz + a
                u = FOUR_PI * jnp.concatenate(tiles[4 * a : 4 * a + 4], axis=0) / diag[z]
                u_out[p, z] = u
                if bz == 3:
                    up_out[(p * 2 + a) * GY : (p * 2 + a + 1) * GY] = u
                if z == 0:
                    down_out[p * GY : (p + 1) * GY] = u
    up_out[LOCAL * 2 * GY :] = plane_of(kappa, GZ - 1)


def inner_kernel(row, up, u_ref, kappa, pick, up_out, w_out, sums_out):
    sel = onehot(iota((SLOTS, CELLS), 0) == positions(row[...]))
    pick[...] = sel.astype(F32).T.astype(BF16)
    up_out[...] = up[...]
    diag = [6.0 + plane_of(kappa, z) for z in range(GZ)]
    inverse = [1.0 / d for d in diag]
    rows = []
    for p in range(LOCAL):
        gamma = delta = eps = cross = jnp.zeros((GY, 128), F32)
        before = jnp.zeros((GY, 128), F32)
        for z in range(GZ):
            centre = u_ref[p, z]
            scaled = diag[z] * centre
            gamma += scaled * centre
            image = scaled - beside_xy(centre)
            if z > 0:
                image = image - u_ref[p, z - 1]
            if z < GZ - 1:
                image = image - u_ref[p, z + 1]
            if z in (0, GZ - 1):
                w_out[p, z] = image
                continue
            w = image * inverse[z]
            w_out[p, z] = w
            delta += centre * image
            eps += image * w
            cross += w * (beside_xy(w) + 2.0 * before)
            before = w
        rows += [jnp.sum(v, axis=0, keepdims=True) for v in (gamma, delta, eps, eps - cross)]
    sums_out[...] = jnp.concatenate(rows, axis=0)


def outer_kernel(inner, u_ref, w_ref, part, up, down, kappa, ends, sums_out):
    keep = inner[0].astype(F32)
    inverse = [1.0 / (6.0 + k) for k in (up[LOCAL * 2 * GY :], plane_of(kappa, 0), plane_of(kappa, GZ - 1))]
    rows = []
    for p in range(LOCAL):
        far, near = (up[(p * 2 + a) * GY : (p * 2 + a + 1) * GY] for a in range(2))
        low, high = u_ref[p, 0], u_ref[p, GZ - 1]
        w_before = keep * (near - (far + low + beside_xy(near)) * inverse[0])
        q_low = w_ref[p, 0] - near
        q_high = w_ref[p, GZ - 1] - down[p * GY : (p + 1) * GY]
        w_low, w_high = q_low * inverse[1], q_high * inverse[2]
        ends[p, 0] = w_low
        ends[p, 1] = w_high
        delta = low * q_low + high * q_high
        eps = q_low * w_low + q_high * w_high
        cross = w_low * (beside_xy(w_low) + 2.0 * (w_before + w_ref[p, 1]))
        cross += w_high * (beside_xy(w_high) + 2.0 * w_ref[p, GZ - 2])
        rows += [jnp.zeros((1, 128), F32)]
        rows += [jnp.sum(v, axis=0, keepdims=True) for v in (delta, eps, eps - cross)]
    sums = jnp.sum(jnp.concatenate(rows, axis=0) + part[...], axis=1, keepdims=True)
    spread = jnp.where(iota((16, 128), 1) == iota((16, 128), 0), sums, 0.0)
    sums_out[...] = jnp.broadcast_to(jnp.sum(spread, axis=0, keepdims=True), (LANES, 128))


def finish_kernel(sums, u_ref, w_ref, ends, number, potential, out, bricks):
    total = jnp.sum(sums[...], axis=0, keepdims=True)
    lane = iota((1, 128), 1)
    for p in range(LOCAL):
        gamma, delta, eps, zeta = (
            jnp.sum(jnp.where(lane == 4 * p + k, total, 0.0), axis=1, keepdims=True) for k in range(4)
        )
        alpha = gamma / delta
        fresh = alpha * alpha * eps - gamma
        grow = 1.0 + fresh / gamma
        energy = grow * grow * delta - 2.0 * grow * alpha * eps + alpha * alpha * zeta
        later = fresh / energy
        on_u = jnp.broadcast_to(alpha + later * grow, (GY, 128))
        on_w = jnp.broadcast_to(later * alpha, (GY, 128))
        for bz in range(4):
            tiles = []
            for a in range(2):
                z = 2 * bz + a
                w = ends[p, z // (GZ - 1)] if z in (0, GZ - 1) else w_ref[p, z]
                x = on_u * u_ref[p, z] - on_w * w
                for c in range(4):
                    tile = x[8 * c : 8 * c + 8]
                    potential[p, z, pl.ds(c, 8, stride=4), :] = tile
                    tiles.append(tile)
            for bx, tile in enumerate(swap_groups(tiles)):
                bricks[p, pl.ds(bz * 64 + bx, 8, stride=8), :] = tile
    wanted = number[...].astype(F32).astype(I32)
    lane = iota((SLOTS, 128), 1)
    sel = onehot(jnp.concatenate([wanted == lane, wanted == lane + 128], axis=1))
    for p in range(LOCAL):
        out[:, p * 128 : (p + 1) * 128] = dot(sel, bricks[p].astype(BF16)).astype(BF16)


def cells_kernel(first, second, pick, returned, head, tail):
    half = CELLS // 2
    cellv = dot(pick[...], returned[...]).astype(BF16)
    head[:half] = cellv[:half]
    tail[...] = cellv[half:]
    lane = iota((META, WIDE), 1)
    orbitals = jnp.zeros((META, WIDE), I32)
    for p in range(LOCAL):
        orbitals = jnp.where(lane == 2 * p, first[p], orbitals)
        orbitals = jnp.where(lane == 2 * p + 1, second[p], orbitals)
    head[half:] = orbitals.astype(F32).astype(BF16)


def terms_kernel(blocks, started, wanted, up, psi, *refs):
    half = CELLS // 2
    parts, refs = refs[: 2 * blocks], refs[2 * blocks :]
    totals, (meta, scalars, sem) = refs[:-3], refs[-3:]
    if started:
        earlier, totals = totals[: len(totals) // 2], totals[len(totals) // 2 :]
    for i in range(blocks):
        meta[i : i + 1] = parts[2 * i][half:, :128].astype(F32).astype(I32)[0:1]
    copy = pltpu.make_async_copy(meta, scalars, sem)
    copy.start()
    for k, total in enumerate(totals):
        total[...] = earlier[k][...] if started else jnp.zeros_like(total)
    copy.wait()
    for i in range(blocks):
        for p in range(LOCAL):
            for k, total in enumerate(totals):

                @pl.when(scalars[i, 2 * p] == wanted[k])
                def _():
                    orbital = psi[scalars[i, 2 * p + 1]].astype(F32)
                    cut = slice(p * 128, (p + 1) * 128)
                    low = dot_nt(up[...], parts[2 * i][:half, cut])
                    high = dot_nt(up[...], parts[2 * i + 1][:, cut])
                    total[...] += jnp.concatenate([low, high], axis=1) * orbital


def add_terms(parts, wanted, up, psi, earlier, count):
    total = jax.ShapeDtypeStruct((NODES_W, CELLS), F32)
    return call(
        functools.partial(terms_kernel, len(parts) // 2, bool(earlier)),
        (total,) * count,
        [SMEM] + [VMEM] * (2 + len(parts) + len(earlier)),
        (wanted, up, psi, *parts, *earlier),
        [pltpu.VMEM((8, 128), I32), pltpu.SMEM((8, 128), I32), pltpu.SemaphoreType.DMA],
    )


def on_device(psi, kappa, interp_down, interp_up, brick_of_cell, pair_first, pair_second):
    struct = jax.ShapeDtypeStruct
    field = struct((LOCAL, GZ, GY, GX), F32)
    row = brick_of_cell.reshape(1, CELLS)
    out = call(
        pack_kernel,
        struct((SLOTS, WIDE + 128), BF16),
        [SMEM, SMEM, VMEM, VMEM, VMEM],
        (pair_first, pair_second, row, interp_down.T, psi),
    )
    arrived = lax.all_to_all(out, "mesh", 0, 0, tiled=True)
    u, up, down, number = call(
        place_kernel,
        (
            field,
            struct(((LOCAL * 2 + 1) * GY, GX), F32),
            struct((LOCAL * GY, GX), F32),
            struct((SLOTS, 128), BF16),
        ),
        [VMEM, VMEM],
        (arrived, kappa),
        [pltpu.VMEM((LOCAL, CELLS, NODES_E), F32)],
    )
    up = lax.ppermute(up, "mesh", [(i, i + 1) for i in range(LANES - 1)])
    down = lax.ppermute(down, "mesh", [(i + 1, i) for i in range(LANES - 1)])
    inner = (lax.axis_index("mesh") > 0).astype(I32).reshape(1)
    pick, upward, w, part = call(
        inner_kernel,
        (
            struct((CELLS, SLOTS), BF16),
            struct((NODES_W, NODES_E), BF16),
            field,
            struct((16, 128), F32),
        ),
        [VMEM, VMEM, VMEM, VMEM],
        (row, interp_up, u, kappa),
    )
    ends, sums = call(
        outer_kernel,
        (struct((LOCAL, 2, GY, GX), F32), struct((LANES, 128), F32)),
        [SMEM, VMEM, VMEM, VMEM, VMEM, VMEM, VMEM],
        (inner, u, w, part, up, down, kappa),
    )
    sums = lax.all_to_all(sums, "mesh", 0, 0, tiled=True)
    potential, back = call(
        finish_kernel,
        (field, struct((SLOTS, WIDE), BF16)),
        [VMEM, VMEM, VMEM, VMEM, VMEM],
        (sums, u, w, ends, number),
        [pltpu.VMEM((LOCAL, CELLS, NODES_E), F32)],
    )
    returned = lax.all_to_all(back, "mesh", 0, 0, tiled=True)
    half = CELLS // 2
    head, tail = call(
        cells_kernel,
        (struct((half + META, WIDE), BF16), struct((half, WIDE), BF16)),
        [SMEM, SMEM, VMEM, VMEM],
        (pair_first, pair_second, pick, returned),
    )

    def along_x(value, by):
        return lax.ppermute(value, "pair", [(i, (i + by) % ORB) for i in range(ORB)])

    right_head, left_tail = along_x(head, 2), along_x(tail, -2)
    right_tail, left_head = along_x(tail, 2), along_x(head, -2)
    across = (along_x(right_head, 2), along_x(left_tail, -2))
    me = lax.axis_index("pair").astype(I32)
    mine, others = me.reshape(1), (me ^ 1).reshape(1)
    both = jnp.concatenate([mine, others])
    sums = add_terms((head, tail), both, upward, psi, (), 2)
    beside = (right_head, right_tail, left_head, left_tail)
    own, other = add_terms(beside, both, upward, psi, sums, 2)
    (other,) = add_terms(across, others, upward, psi, (other,), 1)
    given = lax.ppermute(other, "pair", [(i, i ^ 1) for i in range(ORB)])
    (own,) = add_terms(across, mine, upward, psi, (own,), 1)
    return potential, (own + given)[None]


def solution(mesh):
    return jax.shard_map(
        on_device,
        mesh=mesh,
        in_specs=(
            P(None, None, "mesh"),
            P("mesh", None, None),
            P(),
            P(),
            P("mesh"),
            P("pair"),
            P("pair"),
        ),
        out_specs=(P("pair", "mesh", None, None), P("pair", None, "mesh")),
        check_vma=False,
    )
```

```python
import functools
import math

import jax
import jax.numpy as jnp
from jax import lax
from jax.experimental import pallas as pl
from jax.experimental.pallas import tpu as pltpu
from jax.sharding import PartitionSpec as P

F32 = jnp.float32
BF16 = jnp.bfloat16
I32 = jnp.int32
FOUR_PI = 4.0 * math.pi

LANES = 32
BOUND = 16
CELLS = 256
SLOTS = LANES * BOUND
NODES_W = 343
NODES_E = 128
LOCAL = 4
ORB = 8
GZ, GY, GX = 8, 32, 128
WIDE = LOCAL * NODES_E
NUMBERS = 8
META = 16

VMEM = pl.BlockSpec(memory_space=pltpu.VMEM)
SMEM = pl.BlockSpec(memory_space=pltpu.SMEM)
PARAMS = pltpu.CompilerParams(vmem_limit_bytes=40 * 1024 * 1024)


def iota(shape, dim):
    return lax.broadcasted_iota(I32, shape, dim)


def onehot(condition):
    return jnp.where(condition, 1.0, 0.0).astype(BF16)


def dot(left, right):
    return lax.dot_general(left, right, (((1,), (0,)), ((), ())), preferred_element_type=F32)


def dot_nt(left, right):
    return lax.dot_general(left, right, (((1,), (1,)), ((), ())), preferred_element_type=F32)


def dot_tn(left, right):
    return lax.dot_general(left, right, (((0,), (0,)), ((), ())), preferred_element_type=F32)


def call(body, out, specs, args, scratch=(), flops=10**7):
    return pl.pallas_call(
        body,
        out_shape=out,
        in_specs=specs,
        out_specs=jax.tree.map(lambda _: VMEM, out),
        scratch_shapes=list(scratch),
        compiler_params=PARAMS,
        cost_estimate=pl.CostEstimate(flops=flops, bytes_accessed=2**21, transcendentals=0),
    )(*args)


def swap_groups(tiles):
    group = iota((8, 128), 1) >> 4
    for bit in (1, 2, 4):
        low = (group & bit) == 0
        mixed = list(tiles)
        for i in range(8):
            if i & bit == 0:
                j = i | bit
                mixed[i] = jnp.where(low, tiles[i], pltpu.roll(tiles[j], 16 * bit, 1))
                mixed[j] = jnp.where(low, pltpu.roll(tiles[i], 128 - 16 * bit, 1), tiles[j])
        tiles = mixed
    return tiles


def plane_of(kappa, z):
    return jnp.concatenate([kappa[z, pl.ds(c, 8, stride=4), :] for c in range(4)], axis=0)


def beside_xy(plane):
    row, lane = iota((8, 128), 0), iota((GY, 128), 1)
    first, last = plane[0:8], plane[24:32]
    above = jnp.where(row < 7, pltpu.roll(first, 7, 0), 0.0)
    below = jnp.where(row > 0, pltpu.roll(last, 1, 0), 0.0)
    along_y = jnp.concatenate([plane[8:32], above], axis=0) + jnp.concatenate(
        [below, plane[0:24]], axis=0
    )
    right = jnp.where(lane < 127, pltpu.roll(plane, 127, 1), 0.0)
    left = jnp.where(lane > 0, pltpu.roll(plane, 1, 1), 0.0)
    return along_y + right + left


def positions(row):
    target = row >> 8
    member = iota((LANES, CELLS), 0) == target
    order = onehot(iota((CELLS, CELLS), 0) < iota((CELLS, CELLS), 1))
    rank = jnp.where(member, dot(onehot(member), order), 0.0)
    return target, member, jnp.sum(rank, axis=0, keepdims=True).astype(I32)


def slots_of(row):
    target, _, rank = positions(row)
    return iota((SLOTS, CELLS), 0) == target * BOUND + rank


def pack_kernel(first, second, row, down, psi, out):
    target, member, rank = positions(row[...])
    sel = onehot(iota((SLOTS, CELLS), 0) == target * BOUND + rank)
    for p in range(LOCAL):
        left, right = psi[first[p]].astype(F32), psi[second[p]].astype(F32)
        rho = dot_tn(down[...], (left * right).astype(BF16)).astype(BF16)
        sent = dot_nt(sel, rho).astype(BF16)
        out[:, p * BOUND : (p + 1) * BOUND] = sent.reshape(LANES, BOUND, NODES_E)
    number = jnp.where(member, (row[...] & 255) - CELLS, 0).astype(F32).astype(BF16)
    lanes = onehot(iota((NODES_E, CELLS), 0) == rank)
    number = dot_nt(number, lanes) + float(CELLS)
    number = jnp.broadcast_to(number[:, None], (LANES, NUMBERS, NODES_E))
    out[:, LOCAL * BOUND :] = number.astype(BF16)


def place_kernel(arrived, kappa, u_out, up_out, down_out, number_out, placed):
    rows = arrived[:, LOCAL * BOUND :].astype(F32).reshape(LANES * NUMBERS, NODES_E).astype(BF16)
    rows = dot(onehot(iota((LANES, rows.shape[0]), 1) == NUMBERS * iota((LANES, rows.shape[0]), 0)), rows)
    rank = onehot(iota((NODES_E, SLOTS), 0) == (iota((NODES_E, SLOTS), 1) & (BOUND - 1)))
    sender = iota((LANES, SLOTS), 0) == (iota((LANES, SLOTS), 1) >> 4)
    number = jnp.where(sender, dot(rows.astype(BF16), rank), 0.0)
    number = jnp.sum(number, axis=0, keepdims=True).astype(I32)
    number_out[...] = number
    sel = onehot(iota((CELLS, SLOTS), 0) == number)
    for p in range(LOCAL):
        placed[p] = dot(sel, arrived[:, p * BOUND : (p + 1) * BOUND].reshape(SLOTS, NODES_E))
    diag = [6.0 + plane_of(kappa, z) for z in range(GZ)]
    for bz in range(4):
        for p in range(LOCAL):
            tiles = swap_groups(
                [placed[p, pl.ds(bz * 64 + bx, 8, stride=8), :] for bx in range(8)]
            )
            for a in range(2):
                z = 2 * bz + a
                u = FOUR_PI * jnp.concatenate(tiles[4 * a : 4 * a + 4], axis=0) / diag[z]
                u_out[p, z] = u
                if bz == 3:
                    up_out[(p * 2 + a) * GY : (p * 2 + a + 1) * GY] = u
                if z == 0:
                    down_out[p * GY : (p + 1) * GY] = u
    up_out[LOCAL * 2 * GY :] = plane_of(kappa, GZ - 1)


def inner_kernel(row, number, up, u_ref, kappa, pick, spread, up_out, w_out, sums_out):
    pick[...] = jnp.where(slots_of(row[...]), 1.0, 0.0).T.astype(BF16)
    sel = iota((CELLS, SLOTS), 0) == number[...]
    spread[...] = jnp.where(sel, 1.0, 0.0).T.astype(BF16)
    up_out[...] = up[...]
    diag = [6.0 + plane_of(kappa, z) for z in range(GZ)]
    inverse = [1.0 / d for d in diag]
    rows = []
    for p in range(LOCAL):
        gamma = delta = eps = cross = jnp.zeros((GY, 128), F32)
        before = jnp.zeros((GY, 128), F32)
        for z in range(GZ):
            centre = u_ref[p, z]
            scaled = diag[z] * centre
            gamma += scaled * centre
            image = scaled - beside_xy(centre)
            if z > 0:
                image = image - u_ref[p, z - 1]
            if z < GZ - 1:
                image = image - u_ref[p, z + 1]
            if z in (0, GZ - 1):
                w_out[p, z] = image
                continue
            w = image * inverse[z]
            w_out[p, z] = w
            delta += centre * image
            eps += image * w
            cross += w * (beside_xy(w) + 2.0 * before)
            before = w
        rows += [jnp.sum(v, axis=0, keepdims=True) for v in (gamma, delta, eps, eps - cross)]
    sums_out[...] = jnp.concatenate(rows, axis=0)


def outer_kernel(inner, u_ref, w_ref, part, up, down, kappa, ends, sums_out):
    keep = inner[0].astype(F32)
    inverse = [1.0 / (6.0 + k) for k in (up[LOCAL * 2 * GY :], plane_of(kappa, 0), plane_of(kappa, GZ - 1))]
    rows = []
    for p in range(LOCAL):
        far, near = (up[(p * 2 + a) * GY : (p * 2 + a + 1) * GY] for a in range(2))
        low, high = u_ref[p, 0], u_ref[p, GZ - 1]
        w_before = keep * (near - (far + low + beside_xy(near)) * inverse[0])
        q_low = w_ref[p, 0] - near
        q_high = w_ref[p, GZ - 1] - down[p * GY : (p + 1) * GY]
        w_low, w_high = q_low * inverse[1], q_high * inverse[2]
        ends[p, 0] = w_low
        ends[p, 1] = w_high
        delta = low * q_low + high * q_high
        eps = q_low * w_low + q_high * w_high
        cross = w_low * (beside_xy(w_low) + 2.0 * (w_before + w_ref[p, 1]))
        cross += w_high * (beside_xy(w_high) + 2.0 * w_ref[p, GZ - 2])
        rows += [jnp.zeros((1, 128), F32)]
        rows += [jnp.sum(v, axis=0, keepdims=True) for v in (delta, eps, eps - cross)]
    sums = jnp.sum(jnp.concatenate(rows, axis=0) + part[...], axis=1, keepdims=True)
    spread = jnp.where(iota((16, 128), 1) == iota((16, 128), 0), sums, 0.0)
    sums_out[...] = jnp.broadcast_to(jnp.sum(spread, axis=0, keepdims=True), (LANES, 128))


def finish_kernel(sums, u_ref, w_ref, ends, spread, potential, out, bricks):
    total = jnp.sum(sums[...], axis=0, keepdims=True)
    lane = iota((1, 128), 1)
    for p in range(LOCAL):
        gamma, delta, eps, zeta = (
            jnp.sum(jnp.where(lane == 4 * p + k, total, 0.0), axis=1, keepdims=True) for k in range(4)
        )
        alpha = gamma / delta
        fresh = alpha * alpha * eps - gamma
        grow = 1.0 + fresh / gamma
        energy = grow * grow * delta - 2.0 * grow * alpha * eps + alpha * alpha * zeta
        later = fresh / energy
        on_u = jnp.broadcast_to(alpha + later * grow, (GY, 128))
        on_w = jnp.broadcast_to(later * alpha, (GY, 128))
        for bz in range(4):
            tiles = []
            for a in range(2):
                z = 2 * bz + a
                w = ends[p, z // (GZ - 1)] if z in (0, GZ - 1) else w_ref[p, z]
                x = on_u * u_ref[p, z] - on_w * w
                for c in range(4):
                    tile = x[8 * c : 8 * c + 8]
                    potential[p, z, pl.ds(c, 8, stride=4), :] = tile
                    tiles.append(tile)
            for bx, tile in enumerate(swap_groups(tiles)):
                bricks[p, pl.ds(bz * 64 + bx, 8, stride=8), :] = tile
    for p in range(LOCAL):
        out[:, p * 128 : (p + 1) * 128] = dot(spread[...], bricks[p].astype(BF16)).astype(BF16)


def cells_kernel(first, second, pick, returned, out):
    out[:CELLS] = dot(pick[...], returned[...]).astype(BF16)
    lane = iota((META, WIDE), 1)
    orbitals = jnp.zeros((META, WIDE), I32)
    for p in range(LOCAL):
        orbitals = jnp.where(lane == 2 * p, first[p], orbitals)
        orbitals = jnp.where(lane == 2 * p + 1, second[p], orbitals)
    out[CELLS:] = orbitals.astype(F32).astype(BF16)


def terms_kernel(started, wanted, up, psi, block, *refs):
    totals, (meta, scalars, sem) = refs[:-3], refs[-3:]
    if started:
        earlier, totals = totals[: len(totals) // 2], totals[len(totals) // 2 :]
    meta[...] = block[CELLS:, :128].astype(F32).astype(I32)[0:8]
    copy = pltpu.make_async_copy(meta, scalars, sem)
    copy.start()
    for k, total in enumerate(totals):
        total[...] = earlier[k][...] if started else jnp.zeros_like(total)
    copy.wait()
    for p in range(LOCAL):
        for k, total in enumerate(totals):

            @pl.when(scalars[0, 2 * p] == wanted[k])
            def _():
                orbital = psi[scalars[0, 2 * p + 1]].astype(F32)
                cellv = block[:CELLS, p * 128 : (p + 1) * 128]
                total[...] += dot_nt(up[...], cellv) * orbital


def add_terms(block, wanted, up, psi, earlier, count):
    total = jax.ShapeDtypeStruct((NODES_W, CELLS), F32)
    return call(
        functools.partial(terms_kernel, bool(earlier)),
        (total,) * count,
        [SMEM] + [VMEM] * (3 + len(earlier)),
        (wanted, up, psi, block, *earlier),
        [pltpu.VMEM((8, 128), I32), pltpu.SMEM((8, 128), I32), pltpu.SemaphoreType.DMA],
    )


def join_kernel(own, given, out):
    total = own[...] + given[...]
    out[:, 0, :] = total[:, :128]
    out[:, 1, :] = total[:, 128:]


def on_device(psi, kappa, interp_down, interp_up, brick_of_cell, pair_first, pair_second):
    struct = jax.ShapeDtypeStruct
    field = struct((LOCAL, GZ, GY, GX), F32)
    row = brick_of_cell.reshape(1, CELLS)
    out = call(
        pack_kernel,
        struct((LANES, LOCAL * BOUND + NUMBERS, NODES_E), BF16),
        [SMEM, SMEM, VMEM, VMEM, VMEM],
        (pair_first, pair_second, row, interp_down.T, psi),
    )
    arrived = lax.all_to_all(out, "mesh", 0, 0, tiled=True)
    u, up, down, number = call(
        place_kernel,
        (
            field,
            struct(((LOCAL * 2 + 1) * GY, GX), F32),
            struct((LOCAL * GY, GX), F32),
            struct((1, SLOTS), I32),
        ),
        [VMEM, VMEM],
        (arrived, kappa),
        [pltpu.VMEM((LOCAL, CELLS, NODES_E), F32)],
    )
    up = lax.ppermute(up, "mesh", [(i, i + 1) for i in range(LANES - 1)])
    down = lax.ppermute(down, "mesh", [(i + 1, i) for i in range(LANES - 1)])
    inner = (lax.axis_index("mesh") > 0).astype(I32).reshape(1)
    pick, spread, upward, w, part = call(
        inner_kernel,
        (
            struct((CELLS, SLOTS), BF16),
            struct((SLOTS, CELLS), BF16),
            struct((NODES_W, NODES_E), BF16),
            field,
            struct((16, 128), F32),
        ),
        [VMEM, VMEM, VMEM, VMEM, VMEM],
        (row, number, interp_up, u, kappa),
    )
    ends, sums = call(
        outer_kernel,
        (struct((LOCAL, 2, GY, GX), F32), struct((LANES, 128), F32)),
        [SMEM, VMEM, VMEM, VMEM, VMEM, VMEM, VMEM],
        (inner, u, w, part, up, down, kappa),
    )
    sums = lax.all_to_all(sums, "mesh", 0, 0, tiled=True)
    potential, back = call(
        finish_kernel,
        (field, struct((SLOTS, WIDE), BF16)),
        [VMEM, VMEM, VMEM, VMEM, VMEM],
        (sums, u, w, ends, spread),
        [pltpu.VMEM((LOCAL, CELLS, NODES_E), F32)],
    )
    returned = lax.all_to_all(back, "mesh", 0, 0, tiled=True)
    value = call(
        cells_kernel,
        struct((CELLS + META, WIDE), BF16),
        [SMEM, SMEM, VMEM, VMEM],
        (pair_first, pair_second, pick, returned),
    )

    def along_x(value, by):
        return lax.ppermute(value, "pair", [(i, (i + by) % ORB) for i in range(ORB)])

    right, left, across = (along_x(value, by) for by in (2, -2, 4))
    me = lax.axis_index("pair").astype(I32)
    mine, others = me.reshape(1), (me ^ 1).reshape(1)
    both = jnp.concatenate([mine, others])
    sums = ()
    for block in (value, left, across):
        sums = add_terms(block, both, upward, psi, sums, 2)
    own, other = sums
    (other,) = add_terms(right, others, upward, psi, (other,), 1)
    given = lax.ppermute(other, "pair", [(i, i ^ 1) for i in range(ORB)])
    (own,) = add_terms(right, mine, upward, psi, (own,), 1)
    action = call(
        join_kernel, struct((NODES_W, 2, CELLS // 2), F32), [VMEM, VMEM], (own, given)
    )
    return potential, action.reshape(1, NODES_W, CELLS)


def solution(mesh):
    return jax.shard_map(
        on_device,
        mesh=mesh,
        in_specs=(
            P(None, None, "mesh"),
            P("mesh", None, None),
            P(),
            P(),
            P("mesh"),
            P("pair"),
            P("pair"),
        ),
        out_specs=(P("pair", "mesh", None, None), P("pair", None, "mesh")),
        check_vma=False,
    )
```

```python
import functools
import math

import jax
import jax.numpy as jnp
from jax import lax
from jax.experimental import pallas as pl
from jax.experimental.pallas import tpu as pltpu
from jax.sharding import PartitionSpec as P

F32 = jnp.float32
BF16 = jnp.bfloat16
I32 = jnp.int32
FOUR_PI = 4.0 * math.pi

LANES = 32
BOUND = 16
CELLS = 256
SLOTS = LANES * BOUND
NODES_W = 343
NODES_E = 128
LOCAL = 4
ORB = 8
GZ, GY, GX = 8, 32, 128
WIDE = LOCAL * NODES_E
NUMBERS = 8
META = 8

VMEM = pl.BlockSpec(memory_space=pltpu.VMEM)
SMEM = pl.BlockSpec(memory_space=pltpu.SMEM)
PARAMS = pltpu.CompilerParams(vmem_limit_bytes=40 * 1024 * 1024)


def iota(shape, dim):
    return lax.broadcasted_iota(I32, shape, dim)


def onehot(condition):
    return jnp.where(condition, 1.0, 0.0).astype(BF16)


def dot(left, right):
    return lax.dot_general(left, right, (((1,), (0,)), ((), ())), preferred_element_type=F32)


def dot_nt(left, right):
    return lax.dot_general(left, right, (((1,), (1,)), ((), ())), preferred_element_type=F32)


def dot_tn(left, right):
    return lax.dot_general(left, right, (((0,), (0,)), ((), ())), preferred_element_type=F32)


def call(body, out, specs, args, scratch=(), flops=10**7):
    return pl.pallas_call(
        body,
        out_shape=out,
        in_specs=specs,
        out_specs=jax.tree.map(lambda _: VMEM, out),
        scratch_shapes=list(scratch),
        compiler_params=PARAMS,
        cost_estimate=pl.CostEstimate(flops=flops, bytes_accessed=2**21, transcendentals=0),
    )(*args)


def swap_groups(tiles):
    group = iota((8, 128), 1) >> 4
    for bit in (1, 2, 4):
        low = (group & bit) == 0
        mixed = list(tiles)
        for i in range(8):
            if i & bit == 0:
                j = i | bit
                mixed[i] = jnp.where(low, tiles[i], pltpu.roll(tiles[j], 16 * bit, 1))
                mixed[j] = jnp.where(low, pltpu.roll(tiles[i], 128 - 16 * bit, 1), tiles[j])
        tiles = mixed
    return tiles


def plane_of(kappa, z):
    return jnp.concatenate([kappa[z, pl.ds(c, 8, stride=4), :] for c in range(4)], axis=0)


def beside_xy(plane):
    row, lane = iota((8, 128), 0), iota((GY, 128), 1)
    first, last = plane[0:8], plane[24:32]
    above = jnp.where(row < 7, pltpu.roll(first, 7, 0), 0.0)
    below = jnp.where(row > 0, pltpu.roll(last, 1, 0), 0.0)
    along_y = jnp.concatenate([plane[8:32], above], axis=0) + jnp.concatenate(
        [below, plane[0:24]], axis=0
    )
    right = jnp.where(lane < 127, pltpu.roll(plane, 127, 1), 0.0)
    left = jnp.where(lane > 0, pltpu.roll(plane, 1, 1), 0.0)
    return along_y + right + left


def positions(row):
    target = row >> 8
    member = iota((LANES, CELLS), 0) == target
    order = onehot(iota((CELLS, CELLS), 0) < iota((CELLS, CELLS), 1))
    rank = jnp.where(member, dot(onehot(member), order), 0.0)
    return target, member, jnp.sum(rank, axis=0, keepdims=True).astype(I32)


def slots_of(row):
    target, _, rank = positions(row)
    return iota((SLOTS, CELLS), 0) == target * BOUND + rank


def pack_kernel(first, second, row, down, psi, out):
    target, member, rank = positions(row[...])
    sel = onehot(iota((SLOTS, CELLS), 0) == target * BOUND + rank)
    dens = [
        (psi[first[p]].astype(F32) * psi[second[p]].astype(F32)).astype(BF16) for p in range(LOCAL)
    ]
    rho = dot_tn(down[...], jnp.concatenate(dens, axis=1)).astype(BF16)
    rho = jnp.concatenate([rho[:, p * CELLS : (p + 1) * CELLS] for p in range(LOCAL)], axis=0)
    sent = dot_nt(sel, rho).astype(BF16)
    for p in range(LOCAL):
        part = sent[:, p * NODES_E : (p + 1) * NODES_E]
        out[:, p * BOUND : (p + 1) * BOUND] = part.reshape(LANES, BOUND, NODES_E)
    number = jnp.where(member, (row[...] & 255) - CELLS, 0).astype(F32).astype(BF16)
    lanes = onehot(iota((NODES_E, CELLS), 0) == rank)
    number = dot_nt(number, lanes) + float(CELLS)
    number = jnp.broadcast_to(number[:, None], (LANES, NUMBERS, NODES_E))
    out[:, LOCAL * BOUND :] = number.astype(BF16)


def place_kernel(arrived, kappa, u_out, up_out, down_out, number_out, placed):
    rows = arrived[:, LOCAL * BOUND :].astype(F32).reshape(LANES * NUMBERS, NODES_E).astype(BF16)
    rows = dot(onehot(iota((LANES, rows.shape[0]), 1) == NUMBERS * iota((LANES, rows.shape[0]), 0)), rows)
    rank = onehot(iota((NODES_E, SLOTS), 0) == (iota((NODES_E, SLOTS), 1) & (BOUND - 1)))
    sender = iota((LANES, SLOTS), 0) == (iota((LANES, SLOTS), 1) >> 4)
    number = jnp.where(sender, dot(rows.astype(BF16), rank), 0.0)
    number = jnp.sum(number, axis=0, keepdims=True).astype(I32)
    number_out[...] = number
    sel = onehot(iota((CELLS, SLOTS), 0) == number)
    parts = [
        arrived[:, p * BOUND : (p + 1) * BOUND].reshape(SLOTS, NODES_E) for p in range(LOCAL)
    ]
    wide = dot(sel, jnp.concatenate(parts, axis=1))
    for p in range(LOCAL):
        placed[p] = wide[:, p * NODES_E : (p + 1) * NODES_E]
    diag = [6.0 + plane_of(kappa, z) for z in range(GZ)]
    for bz in range(4):
        for p in range(LOCAL):
            tiles = swap_groups(
                [placed[p, pl.ds(bz * 64 + bx, 8, stride=8), :] for bx in range(8)]
            )
            for a in range(2):
                z = 2 * bz + a
                u = FOUR_PI * jnp.concatenate(tiles[4 * a : 4 * a + 4], axis=0) / diag[z]
                u_out[p, z] = u
                if bz == 3:
                    up_out[(p * 2 + a) * GY : (p * 2 + a + 1) * GY] = u
                if z == 0:
                    down_out[p * GY : (p + 1) * GY] = u
    up_out[LOCAL * 2 * GY :] = plane_of(kappa, GZ - 1)


def inner_kernel(row, number, up, u_ref, kappa, pick, spread, up_out, w_out, sums_out):
    pick[...] = jnp.where(slots_of(row[...]), 1.0, 0.0).T.astype(BF16)
    sel = iota((CELLS, SLOTS), 0) == number[...]
    spread[...] = jnp.where(sel, 1.0, 0.0).T.astype(BF16)
    up_out[...] = up[...]
    diag = [6.0 + plane_of(kappa, z) for z in range(GZ)]
    inverse = [1.0 / d for d in diag]
    rows = []
    for p in range(LOCAL):
        gamma = delta = eps = cross = jnp.zeros((GY, 128), F32)
        before = jnp.zeros((GY, 128), F32)
        for z in range(GZ):
            centre = u_ref[p, z]
            scaled = diag[z] * centre
            gamma += scaled * centre
            image = scaled - beside_xy(centre)
            if z > 0:
                image = image - u_ref[p, z - 1]
            if z < GZ - 1:
                image = image - u_ref[p, z + 1]
            if z in (0, GZ - 1):
                w_out[p, z] = image
                continue
            w = image * inverse[z]
            w_out[p, z] = w
            delta += centre * image
            eps += image * w
            cross += w * (beside_xy(w) + 2.0 * before)
            before = w
        rows += [jnp.sum(v, axis=0, keepdims=True) for v in (gamma, delta, eps, eps - cross)]
    sums_out[...] = jnp.concatenate(rows, axis=0)


def outer_kernel(inner, u_ref, w_ref, part, up, down, kappa, ends, sums_out):
    keep = inner[0].astype(F32)
    inverse = [1.0 / (6.0 + k) for k in (up[LOCAL * 2 * GY :], plane_of(kappa, 0), plane_of(kappa, GZ - 1))]
    rows = []
    for p in range(LOCAL):
        far, near = (up[(p * 2 + a) * GY : (p * 2 + a + 1) * GY] for a in range(2))
        low, high = u_ref[p, 0], u_ref[p, GZ - 1]
        w_before = keep * (near - (far + low + beside_xy(near)) * inverse[0])
        q_low = w_ref[p, 0] - near
        q_high = w_ref[p, GZ - 1] - down[p * GY : (p + 1) * GY]
        w_low, w_high = q_low * inverse[1], q_high * inverse[2]
        ends[p, 0] = w_low
        ends[p, 1] = w_high
        delta = low * q_low + high * q_high
        eps = q_low * w_low + q_high * w_high
        cross = w_low * (beside_xy(w_low) + 2.0 * (w_before + w_ref[p, 1]))
        cross += w_high * (beside_xy(w_high) + 2.0 * w_ref[p, GZ - 2])
        rows += [jnp.zeros((1, 128), F32)]
        rows += [jnp.sum(v, axis=0, keepdims=True) for v in (delta, eps, eps - cross)]
    sums = jnp.sum(jnp.concatenate(rows, axis=0) + part[...], axis=1, keepdims=True)
    spread = jnp.where(iota((16, 128), 1) == iota((16, 128), 0), sums, 0.0)
    sums_out[...] = jnp.broadcast_to(jnp.sum(spread, axis=0, keepdims=True), (LANES, 128))


def finish_kernel(sums, u_ref, w_ref, ends, spread, potential, out, bricks):
    total = jnp.sum(sums[...], axis=0, keepdims=True)
    lane = iota((1, 128), 1)
    for p in range(LOCAL):
        gamma, delta, eps, zeta = (
            jnp.sum(jnp.where(lane == 4 * p + k, total, 0.0), axis=1, keepdims=True) for k in range(4)
        )
        alpha = gamma / delta
        fresh = alpha * alpha * eps - gamma
        grow = 1.0 + fresh / gamma
        energy = grow * grow * delta - 2.0 * grow * alpha * eps + alpha * alpha * zeta
        later = fresh / energy
        on_u = jnp.broadcast_to(alpha + later * grow, (GY, 128))
        on_w = jnp.broadcast_to(later * alpha, (GY, 128))
        for bz in range(4):
            tiles = []
            for a in range(2):
                z = 2 * bz + a
                w = ends[p, z // (GZ - 1)] if z in (0, GZ - 1) else w_ref[p, z]
                x = on_u * u_ref[p, z] - on_w * w
                for c in range(4):
                    tile = x[8 * c : 8 * c + 8]
                    potential[p, z, pl.ds(c, 8, stride=4), :] = tile
                    tiles.append(tile)
            for bx, tile in enumerate(swap_groups(tiles)):
                bricks[p, pl.ds(bz * 64 + bx, 8, stride=8), :] = tile
    wide = jnp.concatenate([bricks[p].astype(BF16) for p in range(LOCAL)], axis=1)
    out[...] = dot(spread[...], wide).astype(BF16)


def cells_kernel(first, second, pick, returned, out):
    out[:CELLS] = dot(pick[...], returned[...]).astype(BF16)
    lane = iota((META, WIDE), 1)
    orbitals = jnp.zeros((META, WIDE), I32)
    for p in range(LOCAL):
        orbitals = jnp.where(lane == 2 * p, first[p], orbitals)
        orbitals = jnp.where(lane == 2 * p + 1, second[p], orbitals)
    out[CELLS:] = orbitals.astype(F32).astype(BF16)


def terms_kernel(started, wanted, up, psi, block, *totals):
    if started:
        earlier, totals = totals[: len(totals) // 2], totals[len(totals) // 2 :]
    orbitals = block[CELLS:, :128].astype(F32).astype(I32)
    lane = iota((META, 128), 1)
    read = [jnp.max(jnp.where(lane == k, orbitals, 0)) for k in range(2 * LOCAL)]
    for k, total in enumerate(totals):
        total[...] = earlier[k][...] if started else jnp.zeros_like(total)
    for p in range(LOCAL):
        for k, total in enumerate(totals):

            @pl.when(read[2 * p] == wanted[k])
            def _():
                orbital = psi[read[2 * p + 1]].astype(F32)
                cellv = block[:CELLS, p * 128 : (p + 1) * 128]
                total[...] += dot_nt(up[...], cellv) * orbital


def add_terms(block, wanted, up, psi, earlier, count):
    total = jax.ShapeDtypeStruct((NODES_W, CELLS), F32)
    return call(
        functools.partial(terms_kernel, bool(earlier)),
        (total,) * count,
        [SMEM] + [VMEM] * (3 + len(earlier)),
        (wanted, up, psi, block, *earlier),
    )


def join_kernel(own, given, out):
    total = own[...] + given[...]
    out[:, 0, :] = total[:, :128]
    out[:, 1, :] = total[:, 128:]


def on_device(psi, kappa, interp_down, interp_up, brick_of_cell, pair_first, pair_second):
    struct = jax.ShapeDtypeStruct
    field = struct((LOCAL, GZ, GY, GX), F32)
    row = brick_of_cell.reshape(1, CELLS)
    out = call(
        pack_kernel,
        struct((LANES, LOCAL * BOUND + NUMBERS, NODES_E), BF16),
        [SMEM, SMEM, VMEM, VMEM, VMEM],
        (pair_first, pair_second, row, interp_down.T, psi),
    )
    arrived = lax.all_to_all(out, "mesh", 0, 0, tiled=True)
    u, up, down, number = call(
        place_kernel,
        (
            field,
            struct(((LOCAL * 2 + 1) * GY, GX), F32),
            struct((LOCAL * GY, GX), F32),
            struct((1, SLOTS), I32),
        ),
        [VMEM, VMEM],
        (arrived, kappa),
        [pltpu.VMEM((LOCAL, CELLS, NODES_E), F32)],
    )
    up = lax.ppermute(up, "mesh", [(i, i + 1) for i in range(LANES - 1)])
    down = lax.ppermute(down, "mesh", [(i + 1, i) for i in range(LANES - 1)])
    inner = (lax.axis_index("mesh") > 0).astype(I32).reshape(1)
    pick, spread, upward, w, part = call(
        inner_kernel,
        (
            struct((CELLS, SLOTS), BF16),
            struct((SLOTS, CELLS), BF16),
            struct((NODES_W, NODES_E), BF16),
            field,
            struct((16, 128), F32),
        ),
        [VMEM, VMEM, VMEM, VMEM, VMEM],
        (row, number, interp_up, u, kappa),
    )
    ends, sums = call(
        outer_kernel,
        (struct((LOCAL, 2, GY, GX), F32), struct((LANES, 128), F32)),
        [SMEM, VMEM, VMEM, VMEM, VMEM, VMEM, VMEM],
        (inner, u, w, part, up, down, kappa),
    )
    sums = lax.all_to_all(sums, "mesh", 0, 0, tiled=True)
    potential, back = call(
        finish_kernel,
        (field, struct((SLOTS, WIDE), BF16)),
        [VMEM, VMEM, VMEM, VMEM, VMEM],
        (sums, u, w, ends, spread),
        [pltpu.VMEM((LOCAL, CELLS, NODES_E), F32)],
    )
    returned = lax.all_to_all(back, "mesh", 0, 0, tiled=True)
    value = call(
        cells_kernel,
        struct((CELLS + META, WIDE), BF16),
        [SMEM, SMEM, VMEM, VMEM],
        (pair_first, pair_second, pick, returned),
    )

    def along_x(value, by):
        return lax.ppermute(value, "pair", [(i, (i + by) % ORB) for i in range(ORB)])

    right, left, across = (along_x(value, by) for by in (2, -2, 4))
    me = lax.axis_index("pair").astype(I32)
    mine, others = me.reshape(1), (me ^ 1).reshape(1)
    both = jnp.concatenate([mine, others])
    sums = ()
    for block in (value, left, across):
        sums = add_terms(block, both, upward, psi, sums, 2)
    own, other = sums
    (other,) = add_terms(right, others, upward, psi, (other,), 1)
    given = lax.ppermute(other, "pair", [(i, i ^ 1) for i in range(ORB)])
    (own,) = add_terms(right, mine, upward, psi, (own,), 1)
    action = call(
        join_kernel, struct((NODES_W, 2, CELLS // 2), F32), [VMEM, VMEM], (own, given)
    )
    return potential, action.reshape(1, NODES_W, CELLS)


def solution(mesh):
    return jax.shard_map(
        on_device,
        mesh=mesh,
        in_specs=(
            P(None, None, "mesh"),
            P("mesh", None, None),
            P(),
            P(),
            P("mesh"),
            P("pair"),
            P("pair"),
        ),
        out_specs=(P("pair", "mesh", None, None), P("pair", None, "mesh")),
        check_vma=False,
    )
```

```python
import functools
import math

import jax
import jax.numpy as jnp
from jax import lax
from jax.experimental import pallas as pl
from jax.experimental.pallas import tpu as pltpu
from jax.sharding import PartitionSpec as P

F32 = jnp.float32
BF16 = jnp.bfloat16
I32 = jnp.int32
FOUR_PI = 4.0 * math.pi

LANES = 32
BOUND = 16
CELLS = 256
SLOTS = LANES * BOUND
NODES_W = 343
NODES_E = 128
LOCAL = 4
ORB = 8
GZ, GY, GX = 8, 32, 128
WIDE = LOCAL * NODES_E
NUMBERS = 8
META = 8

VMEM = pl.BlockSpec(memory_space=pltpu.VMEM)
SMEM = pl.BlockSpec(memory_space=pltpu.SMEM)
PARAMS = pltpu.CompilerParams(vmem_limit_bytes=40 * 1024 * 1024)


def iota(shape, dim):
    return lax.broadcasted_iota(I32, shape, dim)


def onehot(condition):
    return jnp.where(condition, 1.0, 0.0).astype(BF16)


def dot(left, right):
    return lax.dot_general(left, right, (((1,), (0,)), ((), ())), preferred_element_type=F32)


def dot_nt(left, right):
    return lax.dot_general(left, right, (((1,), (1,)), ((), ())), preferred_element_type=F32)


def dot_tn(left, right):
    return lax.dot_general(left, right, (((0,), (0,)), ((), ())), preferred_element_type=F32)


def call(body, out, specs, args, scratch=(), flops=10**7):
    return pl.pallas_call(
        body,
        out_shape=out,
        in_specs=specs,
        out_specs=jax.tree.map(lambda _: VMEM, out),
        scratch_shapes=list(scratch),
        compiler_params=PARAMS,
        cost_estimate=pl.CostEstimate(flops=flops, bytes_accessed=2**21, transcendentals=0),
    )(*args)


def swap_groups(tiles):
    group = iota((8, 128), 1) >> 4
    for bit in (1, 2, 4):
        low = (group & bit) == 0
        mixed = list(tiles)
        for i in range(8):
            if i & bit == 0:
                j = i | bit
                mixed[i] = jnp.where(low, tiles[i], pltpu.roll(tiles[j], 16 * bit, 1))
                mixed[j] = jnp.where(low, pltpu.roll(tiles[i], 128 - 16 * bit, 1), tiles[j])
        tiles = mixed
    return tiles


def plane_of(kappa, z):
    return jnp.concatenate([kappa[z, pl.ds(c, 8, stride=4), :] for c in range(4)], axis=0)


def beside_xy(plane):
    row, lane = iota((8, 128), 0), iota((GY, 128), 1)
    first, last = plane[0:8], plane[24:32]
    above = jnp.where(row < 7, pltpu.roll(first, 7, 0), 0.0)
    below = jnp.where(row > 0, pltpu.roll(last, 1, 0), 0.0)
    along_y = jnp.concatenate([plane[8:32], above], axis=0) + jnp.concatenate(
        [below, plane[0:24]], axis=0
    )
    right = jnp.where(lane < 127, pltpu.roll(plane, 127, 1), 0.0)
    left = jnp.where(lane > 0, pltpu.roll(plane, 1, 1), 0.0)
    return along_y + right + left


def positions(row):
    target = row >> 8
    member = iota((LANES, CELLS), 0) == target
    order = onehot(iota((CELLS, CELLS), 0) < iota((CELLS, CELLS), 1))
    rank = jnp.where(member, dot(onehot(member), order), 0.0)
    return target, member, jnp.sum(rank, axis=0, keepdims=True).astype(I32)


def slots_of(row):
    target, _, rank = positions(row)
    return iota((SLOTS, CELLS), 0) == target * BOUND + rank


def pack_kernel(first, second, row, down, psi, out):
    target, member, rank = positions(row[...])
    sel = onehot(iota((SLOTS, CELLS), 0) == target * BOUND + rank)
    dens = [
        (psi[first[p]].astype(F32) * psi[second[p]].astype(F32)).astype(BF16) for p in range(LOCAL)
    ]
    rho = dot_tn(down[...], jnp.concatenate(dens, axis=1)).astype(BF16)
    rho = jnp.concatenate([rho[:, p * CELLS : (p + 1) * CELLS] for p in range(LOCAL)], axis=0)
    sent = dot_nt(sel, rho).astype(BF16)
    for p in range(LOCAL):
        part = sent[:, p * NODES_E : (p + 1) * NODES_E]
        out[:, p * BOUND : (p + 1) * BOUND] = part.reshape(LANES, BOUND, NODES_E)
    number = jnp.where(member, (row[...] & 255) - CELLS, 0).astype(F32).astype(BF16)
    lanes = onehot(iota((NODES_E, CELLS), 0) == rank)
    number = dot_nt(number, lanes) + float(CELLS)
    number = jnp.broadcast_to(number[:, None], (LANES, NUMBERS, NODES_E))
    out[:, LOCAL * BOUND :] = number.astype(BF16)


def place_kernel(arrived, kappa, u_out, up_out, down_out, number_out, placed):
    rows = arrived[:, LOCAL * BOUND :].astype(F32).reshape(LANES * NUMBERS, NODES_E).astype(BF16)
    rows = dot(onehot(iota((LANES, rows.shape[0]), 1) == NUMBERS * iota((LANES, rows.shape[0]), 0)), rows)
    rank = onehot(iota((NODES_E, SLOTS), 0) == (iota((NODES_E, SLOTS), 1) & (BOUND - 1)))
    sender = iota((LANES, SLOTS), 0) == (iota((LANES, SLOTS), 1) >> 4)
    number = jnp.where(sender, dot(rows.astype(BF16), rank), 0.0)
    number = jnp.sum(number, axis=0, keepdims=True).astype(I32)
    number_out[...] = number
    sel = onehot(iota((CELLS, SLOTS), 0) == number)
    parts = [
        arrived[:, p * BOUND : (p + 1) * BOUND].reshape(SLOTS, NODES_E) for p in range(LOCAL)
    ]
    wide = dot(sel, jnp.concatenate(parts, axis=1))
    for p in range(LOCAL):
        placed[p] = wide[:, p * NODES_E : (p + 1) * NODES_E]
    diag = [6.0 + plane_of(kappa, z) for z in range(GZ)]
    for bz in range(4):
        for p in range(LOCAL):
            tiles = swap_groups(
                [placed[p, pl.ds(bz * 64 + bx, 8, stride=8), :] for bx in range(8)]
            )
            for a in range(2):
                z = 2 * bz + a
                u = FOUR_PI * jnp.concatenate(tiles[4 * a : 4 * a + 4], axis=0) / diag[z]
                u_out[p, z] = u
                if bz == 3:
                    up_out[(p * 2 + a) * GY : (p * 2 + a + 1) * GY] = u
                if z == 0:
                    down_out[p * GY : (p + 1) * GY] = u
    up_out[LOCAL * 2 * GY :] = plane_of(kappa, GZ - 1)


def inner_kernel(row, number, up, u_ref, kappa, pick, spread, up_out, w_out, sums_out):
    pick[...] = jnp.where(slots_of(row[...]), 1.0, 0.0).T.astype(BF16)
    sel = iota((CELLS, SLOTS), 0) == number[...]
    spread[...] = jnp.where(sel, 1.0, 0.0).T.astype(BF16)
    up_out[...] = up[...]
    diag = [6.0 + plane_of(kappa, z) for z in range(GZ)]
    inverse = [1.0 / d for d in diag]
    rows = []
    for p in range(LOCAL):
        gamma = delta = eps = cross = jnp.zeros((GY, 128), F32)
        before = jnp.zeros((GY, 128), F32)
        for z in range(GZ):
            centre = u_ref[p, z]
            scaled = diag[z] * centre
            gamma += scaled * centre
            image = scaled - beside_xy(centre)
            if z > 0:
                image = image - u_ref[p, z - 1]
            if z < GZ - 1:
                image = image - u_ref[p, z + 1]
            if z in (0, GZ - 1):
                w_out[p, z] = image
                continue
            w = image * inverse[z]
            w_out[p, z] = w
            delta += centre * image
            eps += image * w
            cross += w * (beside_xy(w) + 2.0 * before)
            before = w
        rows += [jnp.sum(v, axis=0, keepdims=True) for v in (gamma, delta, eps, eps - cross)]
    sums_out[...] = jnp.concatenate(rows, axis=0)


def outer_kernel(inner, u_ref, w_ref, part, up, down, kappa, ends, sums_out):
    keep = inner[0].astype(F32)
    inverse = [1.0 / (6.0 + k) for k in (up[LOCAL * 2 * GY :], plane_of(kappa, 0), plane_of(kappa, GZ - 1))]
    rows = []
    for p in range(LOCAL):
        far, near = (up[(p * 2 + a) * GY : (p * 2 + a + 1) * GY] for a in range(2))
        low, high = u_ref[p, 0], u_ref[p, GZ - 1]
        w_before = keep * (near - (far + low + beside_xy(near)) * inverse[0])
        q_low = w_ref[p, 0] - near
        q_high = w_ref[p, GZ - 1] - down[p * GY : (p + 1) * GY]
        w_low, w_high = q_low * inverse[1], q_high * inverse[2]
        ends[p, 0] = w_low
        ends[p, 1] = w_high
        delta = low * q_low + high * q_high
        eps = q_low * w_low + q_high * w_high
        cross = w_low * (beside_xy(w_low) + 2.0 * (w_before + w_ref[p, 1]))
        cross += w_high * (beside_xy(w_high) + 2.0 * w_ref[p, GZ - 2])
        rows += [jnp.zeros((1, 128), F32)]
        rows += [jnp.sum(v, axis=0, keepdims=True) for v in (delta, eps, eps - cross)]
    sums = jnp.sum(jnp.concatenate(rows, axis=0) + part[...], axis=1, keepdims=True)
    spread = jnp.where(iota((16, 128), 1) == iota((16, 128), 0), sums, 0.0)
    sums_out[...] = jnp.broadcast_to(jnp.sum(spread, axis=0, keepdims=True), (LANES, 128))


def finish_kernel(sums, u_ref, w_ref, ends, spread, potential, out, bricks):
    total = jnp.sum(sums[...], axis=0, keepdims=True)
    lane = iota((1, 128), 1)
    for p in range(LOCAL):
        gamma, delta, eps, zeta = (
            jnp.sum(jnp.where(lane == 4 * p + k, total, 0.0), axis=1, keepdims=True) for k in range(4)
        )
        alpha = gamma / delta
        fresh = alpha * alpha * eps - gamma
        grow = 1.0 + fresh / gamma
        energy = grow * grow * delta - 2.0 * grow * alpha * eps + alpha * alpha * zeta
        later = fresh / energy
        on_u = jnp.broadcast_to(alpha + later * grow, (GY, 128))
        on_w = jnp.broadcast_to(later * alpha, (GY, 128))
        for bz in range(4):
            tiles = []
            for a in range(2):
                z = 2 * bz + a
                w = ends[p, z // (GZ - 1)] if z in (0, GZ - 1) else w_ref[p, z]
                x = on_u * u_ref[p, z] - on_w * w
                for c in range(4):
                    tile = x[8 * c : 8 * c + 8]
                    potential[p, z, pl.ds(c, 8, stride=4), :] = tile
                    tiles.append(tile)
            for bx, tile in enumerate(swap_groups(tiles)):
                bricks[p, pl.ds(bz * 64 + bx, 8, stride=8), :] = tile
    wide = jnp.concatenate([bricks[p].astype(BF16) for p in range(LOCAL)], axis=1)
    out[...] = dot(spread[...], wide).astype(BF16)


def cells_kernel(first, second, pick, returned, out):
    out[:CELLS] = dot(pick[...], returned[...]).astype(BF16)
    lane = iota((META, WIDE), 1)
    orbitals = jnp.zeros((META, WIDE), I32)
    for p in range(LOCAL):
        orbitals = jnp.where(lane == 2 * p, first[p], orbitals)
        orbitals = jnp.where(lane == 2 * p + 1, second[p], orbitals)
    out[CELLS:] = orbitals.astype(F32).astype(BF16)


def terms_kernel(count, started, *refs):
    wanted, (up, psi, block, *totals) = refs[:count], refs[count:]
    if started:
        earlier, totals = totals[:count], totals[count:]
    orbitals = block[CELLS:, :128].astype(F32).astype(I32)
    lane = iota((META, 128), 1)
    read = [jnp.max(jnp.where(lane == k, orbitals, 0)) for k in range(2 * LOCAL)]
    for k, total in enumerate(totals):
        total[...] = earlier[k][...] if started else jnp.zeros_like(total)
    for p in range(LOCAL):
        for k, total in enumerate(totals):

            @pl.when(read[2 * p] == wanted[k][0])
            def _():
                orbital = psi[read[2 * p + 1]].astype(F32)
                cellv = block[:CELLS, p * 128 : (p + 1) * 128]
                total[...] += dot_nt(up[...], cellv) * orbital


def add_terms(block, wanted, up, psi, earlier):
    total = jax.ShapeDtypeStruct((NODES_W, CELLS), F32)
    count = len(wanted)
    return call(
        functools.partial(terms_kernel, count, bool(earlier)),
        (total,) * count,
        [SMEM] * count + [VMEM] * (3 + len(earlier)),
        (*wanted, up, psi, block, *earlier),
    )


def join_kernel(own, given, out):
    total = own[...] + given[...]
    out[:, 0, :] = total[:, :128]
    out[:, 1, :] = total[:, 128:]


def on_device(psi, kappa, interp_down, interp_up, brick_of_cell, pair_first, pair_second):
    struct = jax.ShapeDtypeStruct
    field = struct((LOCAL, GZ, GY, GX), F32)
    row = brick_of_cell.reshape(1, CELLS)
    out = call(
        pack_kernel,
        struct((LANES, LOCAL * BOUND + NUMBERS, NODES_E), BF16),
        [SMEM, SMEM, VMEM, VMEM, VMEM],
        (pair_first, pair_second, row, interp_down.T, psi),
    )
    arrived = lax.all_to_all(out, "mesh", 0, 0, tiled=True)
    u, up, down, number = call(
        place_kernel,
        (
            field,
            struct(((LOCAL * 2 + 1) * GY, GX), F32),
            struct((LOCAL * GY, GX), F32),
            struct((1, SLOTS), I32),
        ),
        [VMEM, VMEM],
        (arrived, kappa),
        [pltpu.VMEM((LOCAL, CELLS, NODES_E), F32)],
    )
    up = lax.ppermute(up, "mesh", [(i, i + 1) for i in range(LANES - 1)])
    down = lax.ppermute(down, "mesh", [(i + 1, i) for i in range(LANES - 1)])
    inner = (lax.axis_index("mesh") > 0).astype(I32).reshape(1)
    pick, spread, upward, w, part = call(
        inner_kernel,
        (
            struct((CELLS, SLOTS), BF16),
            struct((SLOTS, CELLS), BF16),
            struct((NODES_W, NODES_E), BF16),
            field,
            struct((16, 128), F32),
        ),
        [VMEM, VMEM, VMEM, VMEM, VMEM],
        (row, number, interp_up, u, kappa),
    )
    ends, sums = call(
        outer_kernel,
        (struct((LOCAL, 2, GY, GX), F32), struct((LANES, 128), F32)),
        [SMEM, VMEM, VMEM, VMEM, VMEM, VMEM, VMEM],
        (inner, u, w, part, up, down, kappa),
    )
    sums = lax.all_to_all(sums, "mesh", 0, 0, tiled=True)
    potential, back = call(
        finish_kernel,
        (field, struct((SLOTS, WIDE), BF16)),
        [VMEM, VMEM, VMEM, VMEM, VMEM],
        (sums, u, w, ends, spread),
        [pltpu.VMEM((LOCAL, CELLS, NODES_E), F32)],
    )
    returned = lax.all_to_all(back, "mesh", 0, 0, tiled=True)
    value = call(
        cells_kernel,
        struct((CELLS + META, WIDE), BF16),
        [SMEM, SMEM, VMEM, VMEM],
        (pair_first, pair_second, pick, returned),
    )

    def along_x(value, by):
        return lax.ppermute(value, "pair", [(i, (i + by) % ORB) for i in range(ORB)])

    right, left, across = (along_x(value, by) for by in (2, -2, 4))
    me = lax.axis_index("pair").astype(I32)
    mine, others = me.reshape(1), (me ^ 1).reshape(1)
    parts = ()
    for block in (value, left, across):
        parts = add_terms(block, (mine, others), upward, psi, parts)
    own, other = parts
    (other,) = add_terms(right, (others,), upward, psi, (other,))
    given = lax.ppermute(other, "pair", [(i, i ^ 1) for i in range(ORB)])
    (own,) = add_terms(right, (mine,), upward, psi, (own,))
    action = call(
        join_kernel, struct((NODES_W, 2, CELLS // 2), F32), [VMEM, VMEM], (own, given)
    )
    return potential, action.reshape(1, NODES_W, CELLS)


def solution(mesh):
    return jax.shard_map(
        on_device,
        mesh=mesh,
        in_specs=(
            P(None, None, "mesh"),
            P("mesh", None, None),
            P(),
            P(),
            P("mesh"),
            P("pair"),
            P("pair"),
        ),
        out_specs=(P("pair", "mesh", None, None), P("pair", None, "mesh")),
        check_vma=False,
    )
```

```python
import functools
import math

import jax
import jax.numpy as jnp
from jax import lax
from jax.experimental import pallas as pl
from jax.experimental.pallas import tpu as pltpu
from jax.sharding import PartitionSpec as P

F32 = jnp.float32
BF16 = jnp.bfloat16
I32 = jnp.int32
FOUR_PI = 4.0 * math.pi

LANES = 32
BOUND = 16
CELLS = 256
SLOTS = LANES * BOUND
NODES_W = 343
NODES_E = 128
LOCAL = 4
ORB = 8
GZ, GY, GX = 8, 32, 128
WIDE = LOCAL * NODES_E
NUMBERS = 8
META = 8

VMEM = pl.BlockSpec(memory_space=pltpu.VMEM)
SMEM = pl.BlockSpec(memory_space=pltpu.SMEM)
PARAMS = pltpu.CompilerParams(vmem_limit_bytes=16 * 1024 * 1024)


def iota(shape, dim):
    return lax.broadcasted_iota(I32, shape, dim)


def onehot(condition):
    return jnp.where(condition, 1.0, 0.0).astype(BF16)


def dot(left, right):
    return lax.dot_general(left, right, (((1,), (0,)), ((), ())), preferred_element_type=F32)


def dot_nt(left, right):
    return lax.dot_general(left, right, (((1,), (1,)), ((), ())), preferred_element_type=F32)


def dot_tn(left, right):
    return lax.dot_general(left, right, (((0,), (0,)), ((), ())), preferred_element_type=F32)


def call(body, out, specs, args, scratch=(), flops=10**7):
    return pl.pallas_call(
        body,
        out_shape=out,
        in_specs=specs,
        out_specs=jax.tree.map(lambda _: VMEM, out),
        scratch_shapes=list(scratch),
        compiler_params=PARAMS,
        cost_estimate=pl.CostEstimate(flops=flops, bytes_accessed=2**21, transcendentals=0),
    )(*args)


def swap_groups(tiles):
    group = iota((8, 128), 1) >> 4
    for bit in (1, 2, 4):
        low = (group & bit) == 0
        mixed = list(tiles)
        for i in range(8):
            if i & bit == 0:
                j = i | bit
                mixed[i] = jnp.where(low, tiles[i], pltpu.roll(tiles[j], 16 * bit, 1))
                mixed[j] = jnp.where(low, pltpu.roll(tiles[i], 128 - 16 * bit, 1), tiles[j])
        tiles = mixed
    return tiles


def plane_of(kappa, z):
    return jnp.concatenate([kappa[z, pl.ds(c, 8, stride=4), :] for c in range(4)], axis=0)


def beside_xy(plane):
    row, lane = iota((8, 128), 0), iota((GY, 128), 1)
    first, last = plane[0:8], plane[24:32]
    above = jnp.where(row < 7, pltpu.roll(first, 7, 0), 0.0)
    below = jnp.where(row > 0, pltpu.roll(last, 1, 0), 0.0)
    along_y = jnp.concatenate([plane[8:32], above], axis=0) + jnp.concatenate(
        [below, plane[0:24]], axis=0
    )
    right = jnp.where(lane < 127, pltpu.roll(plane, 127, 1), 0.0)
    left = jnp.where(lane > 0, pltpu.roll(plane, 1, 1), 0.0)
    return along_y + right + left


def positions(row):
    target = row >> 8
    member = iota((LANES, CELLS), 0) == target
    order = onehot(iota((CELLS, CELLS), 0) < iota((CELLS, CELLS), 1))
    rank = jnp.where(member, dot(onehot(member), order), 0.0)
    return target, member, jnp.sum(rank, axis=0, keepdims=True).astype(I32)


def slots_of(row):
    target, _, rank = positions(row)
    return iota((SLOTS, CELLS), 0) == target * BOUND + rank


def each(orbitals):
    lane = iota((1, LOCAL), 1)
    return [jnp.max(jnp.where(lane == p, orbitals[...], 0)) for p in range(LOCAL)]


def pack_kernel(first, second, row, down, psi, out):
    target, member, rank = positions(row[...])
    sel = onehot(iota((SLOTS, CELLS), 0) == target * BOUND + rank)
    dens = [
        (psi[a].astype(F32) * psi[b].astype(F32)).astype(BF16)
        for a, b in zip(each(first), each(second))
    ]
    rho = dot_tn(down[...], jnp.concatenate(dens, axis=1)).astype(BF16)
    rho = jnp.concatenate([rho[:, p * CELLS : (p + 1) * CELLS] for p in range(LOCAL)], axis=0)
    sent = dot_nt(sel, rho).astype(BF16)
    for p in range(LOCAL):
        part = sent[:, p * NODES_E : (p + 1) * NODES_E]
        out[:, p * BOUND : (p + 1) * BOUND] = part.reshape(LANES, BOUND, NODES_E)
    number = jnp.where(member, (row[...] & 255) - CELLS, 0).astype(F32).astype(BF16)
    lanes = onehot(iota((NODES_E, CELLS), 0) == rank)
    number = dot_nt(number, lanes) + float(CELLS)
    number = jnp.broadcast_to(number[:, None], (LANES, NUMBERS, NODES_E))
    out[:, LOCAL * BOUND :] = number.astype(BF16)


def placed_bricks(number, arrived, start, count, skip):
    brick = iota((count, SLOTS), 0)
    brick = brick + start + jnp.where(brick >= count // 2, skip, 0)
    parts = [
        arrived[:, p * BOUND : (p + 1) * BOUND].reshape(SLOTS, NODES_E) for p in range(LOCAL)
    ]
    return dot(onehot(brick == number), jnp.concatenate(parts, axis=1))


def two_layers(placed, p, row, diag):
    tiles = swap_groups([placed[p, pl.ds(row + bx, 8, stride=8), :] for bx in range(8)])
    return [
        FOUR_PI * jnp.concatenate(tiles[4 * a : 4 * a + 4], axis=0) / diag[a] for a in range(2)
    ]


def edges_kernel(arrived, kappa, u_out, up_out, down_out, number_out, placed):
    rows = arrived[:, LOCAL * BOUND :].astype(F32).reshape(LANES * NUMBERS, NODES_E).astype(BF16)
    rows = dot(onehot(iota((LANES, rows.shape[0]), 1) == NUMBERS * iota((LANES, rows.shape[0]), 0)), rows)
    rank = onehot(iota((NODES_E, SLOTS), 0) == (iota((NODES_E, SLOTS), 1) & (BOUND - 1)))
    sender = iota((LANES, SLOTS), 0) == (iota((LANES, SLOTS), 1) >> 4)
    number = jnp.where(sender, dot(rows.astype(BF16), rank), 0.0)
    number = jnp.sum(number, axis=0, keepdims=True).astype(I32)
    number_out[...] = number
    wide = placed_bricks(number, arrived, 0, 128, 128)
    for p in range(LOCAL):
        placed[p] = wide[:, p * NODES_E : (p + 1) * NODES_E]
    diag = [6.0 + plane_of(kappa, z) for z in (0, 1, GZ - 2, GZ - 1)]
    for p in range(LOCAL):
        u = two_layers(placed, p, 0, diag[:2]) + two_layers(placed, p, 64, diag[2:])
        for i, plane in enumerate(u):
            u_out[p, i] = plane
        for a in range(2):
            up_out[(p * 2 + a) * GY : (p * 2 + a + 1) * GY] = u[2 + a]
        down_out[p * GY : (p + 1) * GY] = u[0]
    up_out[LOCAL * 2 * GY :] = plane_of(kappa, GZ - 1)


def inner_kernel(first, second, row, number, up, arrived, edges, kappa, pick, spread, orbitals, up_out, u_ref, w_out, sums_out, placed):
    pick[...] = jnp.where(slots_of(row[...]), 1.0, 0.0).T.astype(BF16)
    sel = iota((CELLS, SLOTS), 0) == number[...]
    spread[...] = jnp.where(sel, 1.0, 0.0).T.astype(BF16)
    up_out[...] = up[...]
    lane = iota((META, WIDE), 1)
    numbers = jnp.zeros((META, WIDE), I32)
    for p, (a, b) in enumerate(zip(each(first), each(second))):
        numbers = jnp.where(lane == 2 * p, a, jnp.where(lane == 2 * p + 1, b, numbers))
    orbitals[...] = numbers.astype(F32).astype(BF16)
    diag = [6.0 + plane_of(kappa, z) for z in range(GZ)]
    inverse = [1.0 / d for d in diag]
    wide = placed_bricks(number[...], arrived, 64, 128, 0)
    for p in range(LOCAL):
        placed[p] = wide[:, p * NODES_E : (p + 1) * NODES_E]
    rows = []
    for p in range(LOCAL):
        u = [edges[p, 0], edges[p, 1]]
        u += two_layers(placed, p, 0, diag[2:4]) + two_layers(placed, p, 64, diag[4:6])
        u += [edges[p, 2], edges[p, 3]]
        gamma = delta = eps = cross = jnp.zeros((GY, 128), F32)
        before = jnp.zeros((GY, 128), F32)
        for z in range(GZ):
            centre = u[z]
            u_ref[p, z] = centre
            scaled = diag[z] * centre
            gamma += scaled * centre
            image = scaled - beside_xy(centre)
            if z > 0:
                image = image - u[z - 1]
            if z < GZ - 1:
                image = image - u[z + 1]
            if z in (0, GZ - 1):
                w_out[p, z] = image
                continue
            w = image * inverse[z]
            w_out[p, z] = w
            delta += centre * image
            eps += image * w
            cross += w * (beside_xy(w) + 2.0 * before)
            before = w
        rows += [jnp.sum(v, axis=0, keepdims=True) for v in (gamma, delta, eps, eps - cross)]
    sums_out[...] = jnp.concatenate(rows, axis=0)


def outer_kernel(inner, u_ref, w_ref, part, up, down, kappa, ends, sums_out):
    keep = inner[0].astype(F32)
    inverse = [1.0 / (6.0 + k) for k in (up[LOCAL * 2 * GY :], plane_of(kappa, 0), plane_of(kappa, GZ - 1))]
    rows = []
    for p in range(LOCAL):
        far, near = (up[(p * 2 + a) * GY : (p * 2 + a + 1) * GY] for a in range(2))
        low, high = u_ref[p, 0], u_ref[p, GZ - 1]
        w_before = keep * (near - (far + low + beside_xy(near)) * inverse[0])
        q_low = w_ref[p, 0] - near
        q_high = w_ref[p, GZ - 1] - down[p * GY : (p + 1) * GY]
        w_low, w_high = q_low * inverse[1], q_high * inverse[2]
        ends[p, 0] = w_low
        ends[p, 1] = w_high
        delta = low * q_low + high * q_high
        eps = q_low * w_low + q_high * w_high
        cross = w_low * (beside_xy(w_low) + 2.0 * (w_before + w_ref[p, 1]))
        cross += w_high * (beside_xy(w_high) + 2.0 * w_ref[p, GZ - 2])
        rows += [jnp.zeros((1, 128), F32)]
        rows += [jnp.sum(v, axis=0, keepdims=True) for v in (delta, eps, eps - cross)]
    sums = jnp.sum(jnp.concatenate(rows, axis=0) + part[...], axis=1, keepdims=True)
    spread = jnp.where(iota((16, 128), 1) == iota((16, 128), 0), sums, 0.0)
    sums_out[...] = jnp.broadcast_to(jnp.sum(spread, axis=0, keepdims=True), (LANES, 128))


def finish_kernel(sums, u_ref, w_ref, ends, spread, potential, out, bricks):
    total = jnp.sum(sums[...], axis=0, keepdims=True)
    lane = iota((1, 128), 1)
    for p in range(LOCAL):
        gamma, delta, eps, zeta = (
            jnp.sum(jnp.where(lane == 4 * p + k, total, 0.0), axis=1, keepdims=True) for k in range(4)
        )
        alpha = gamma / delta
        fresh = alpha * alpha * eps - gamma
        grow = 1.0 + fresh / gamma
        energy = grow * grow * delta - 2.0 * grow * alpha * eps + alpha * alpha * zeta
        later = fresh / energy
        on_u = jnp.broadcast_to(alpha + later * grow, (GY, 128))
        on_w = jnp.broadcast_to(later * alpha, (GY, 128))
        for bz in range(4):
            tiles = []
            for a in range(2):
                z = 2 * bz + a
                w = ends[p, z // (GZ - 1)] if z in (0, GZ - 1) else w_ref[p, z]
                x = on_u * u_ref[p, z] - on_w * w
                for c in range(4):
                    tile = x[8 * c : 8 * c + 8]
                    potential[p, z, pl.ds(c, 8, stride=4), :] = tile
                    tiles.append(tile)
            for bx, tile in enumerate(swap_groups(tiles)):
                bricks[p, pl.ds(bz * 64 + bx, 8, stride=8), :] = tile
    wide = jnp.concatenate([bricks[p].astype(BF16) for p in range(LOCAL)], axis=1)
    out[...] = dot(spread[...], wide).astype(BF16)


def cells_kernel(pick, returned, orbitals, out):
    out[:CELLS] = dot(pick[...], returned[...]).astype(BF16)
    out[CELLS:] = orbitals[...]


def terms_kernel(count, started, *refs):
    wanted, (up, psi, block, *totals) = refs[:count], refs[count:]
    if started:
        earlier, totals = totals[:count], totals[count:]
    orbitals = block[CELLS:, :128].astype(F32).astype(I32)
    lane = iota((META, 128), 1)
    read = [jnp.max(jnp.where(lane == k, orbitals, 0)) for k in range(2 * LOCAL)]
    for k, total in enumerate(totals):
        total[...] = earlier[k][...] if started else jnp.zeros_like(total)
    for p in range(LOCAL):
        for k, total in enumerate(totals):

            @pl.when(read[2 * p] == wanted[k][0])
            def _():
                orbital = psi[read[2 * p + 1]].astype(F32)
                cellv = block[:CELLS, p * 128 : (p + 1) * 128]
                total[...] += dot_nt(up[...], cellv) * orbital


def add_terms(block, wanted, up, psi, earlier):
    total = jax.ShapeDtypeStruct((NODES_W, CELLS), F32)
    count = len(wanted)
    return call(
        functools.partial(terms_kernel, count, bool(earlier)),
        (total,) * count,
        [SMEM] * count + [VMEM] * (3 + len(earlier)),
        (*wanted, up, psi, block, *earlier),
    )


def join_kernel(own, given, out):
    total = own[...] + given[...]
    out[:, 0, :] = total[:, :128]
    out[:, 1, :] = total[:, 128:]


def on_device(psi, kappa, interp_down, interp_up, brick_of_cell, pair_first, pair_second):
    struct = jax.ShapeDtypeStruct
    field = struct((LOCAL, GZ, GY, GX), F32)
    row = brick_of_cell.reshape(1, CELLS)
    first, second = pair_first.reshape(1, LOCAL), pair_second.reshape(1, LOCAL)
    out = call(
        pack_kernel,
        struct((LANES, LOCAL * BOUND + NUMBERS, NODES_E), BF16),
        [VMEM] * 5,
        (first, second, row, interp_down.T, psi),
    )
    arrived = lax.all_to_all(out, "mesh", 0, 0, tiled=True)
    half = pltpu.VMEM((LOCAL, CELLS // 2, NODES_E), F32)
    edges, up, down, number = call(
        edges_kernel,
        (
            struct((LOCAL, 4, GY, GX), F32),
            struct(((LOCAL * 2 + 1) * GY, GX), F32),
            struct((LOCAL * GY, GX), F32),
            struct((1, SLOTS), I32),
        ),
        [VMEM, VMEM],
        (arrived, kappa),
        [half],
    )
    up = lax.ppermute(up, "mesh", [(i, i + 1) for i in range(LANES - 1)])
    down = lax.ppermute(down, "mesh", [(i + 1, i) for i in range(LANES - 1)])
    inner = (lax.axis_index("mesh") > 0).astype(I32).reshape(1)
    pick, spread, orbitals, upward, u, w, part = call(
        inner_kernel,
        (
            struct((CELLS, SLOTS), BF16),
            struct((SLOTS, CELLS), BF16),
            struct((META, WIDE), BF16),
            struct((NODES_W, NODES_E), BF16),
            field,
            field,
            struct((16, 128), F32),
        ),
        [VMEM] * 8,
        (first, second, row, number, interp_up, arrived, edges, kappa),
        [half],
    )
    ends, sums = call(
        outer_kernel,
        (struct((LOCAL, 2, GY, GX), F32), struct((LANES, 128), F32)),
        [SMEM, VMEM, VMEM, VMEM, VMEM, VMEM, VMEM],
        (inner, u, w, part, up, down, kappa),
    )
    sums = lax.all_to_all(sums, "mesh", 0, 0, tiled=True)
    potential, back = call(
        finish_kernel,
        (field, struct((SLOTS, WIDE), BF16)),
        [VMEM, VMEM, VMEM, VMEM, VMEM],
        (sums, u, w, ends, spread),
        [pltpu.VMEM((LOCAL, CELLS, NODES_E), F32)],
    )
    returned = lax.all_to_all(back, "mesh", 0, 0, tiled=True)
    value = call(
        cells_kernel,
        struct((CELLS + META, WIDE), BF16),
        [VMEM] * 3,
        (pick, returned, orbitals),
    )

    def along_x(value, by):
        return lax.ppermute(value, "pair", [(i, (i + by) % ORB) for i in range(ORB)])

    right, left, across = (along_x(value, by) for by in (2, -2, 4))
    me = lax.axis_index("pair").astype(I32)
    mine, others = me.reshape(1), (me ^ 1).reshape(1)
    parts = ()
    for block in (value, left, across):
        parts = add_terms(block, (mine, others), upward, psi, parts)
    own, other = parts
    (other,) = add_terms(right, (others,), upward, psi, (other,))
    given = lax.ppermute(other, "pair", [(i, i ^ 1) for i in range(ORB)])
    (own,) = add_terms(right, (mine,), upward, psi, (own,))
    action = call(
        join_kernel, struct((NODES_W, 2, CELLS // 2), F32), [VMEM, VMEM], (own, given)
    )
    return potential, action.reshape(1, NODES_W, CELLS)


def solution(mesh):
    return jax.shard_map(
        on_device,
        mesh=mesh,
        in_specs=(
            P(None, None, "mesh"),
            P("mesh", None, None),
            P(),
            P(),
            P("mesh"),
            P("pair"),
            P("pair"),
        ),
        out_specs=(P("pair", "mesh", None, None), P("pair", None, "mesh")),
        check_vma=False,
    )
```

```python
import functools
import math

import jax
import jax.numpy as jnp
from jax import lax
from jax.experimental import pallas as pl
from jax.experimental.pallas import tpu as pltpu
from jax.sharding import PartitionSpec as P

F32 = jnp.float32
BF16 = jnp.bfloat16
I32 = jnp.int32
FOUR_PI = 4.0 * math.pi

LANES = 32
BOUND = 16
CELLS = 256
SLOTS = LANES * BOUND
NODES_W = 343
NODES_E = 128
LOCAL = 4
ORB = 8
GZ, GY, GX = 8, 32, 128
WIDE = LOCAL * NODES_E
NUMBERS = 8
META = 8

VMEM = pl.BlockSpec(memory_space=pltpu.VMEM)
SMEM = pl.BlockSpec(memory_space=pltpu.SMEM)
PARAMS = pltpu.CompilerParams(vmem_limit_bytes=16 * 1024 * 1024)


def iota(shape, dim):
    return lax.broadcasted_iota(I32, shape, dim)


def onehot(condition):
    return jnp.where(condition, 1.0, 0.0).astype(BF16)


def dot(left, right):
    return lax.dot_general(left, right, (((1,), (0,)), ((), ())), preferred_element_type=F32)


def dot_nt(left, right):
    return lax.dot_general(left, right, (((1,), (1,)), ((), ())), preferred_element_type=F32)


def dot_tn(left, right):
    return lax.dot_general(left, right, (((0,), (0,)), ((), ())), preferred_element_type=F32)


def call(body, out, specs, args, scratch=(), flops=10**7):
    return pl.pallas_call(
        body,
        out_shape=out,
        in_specs=specs,
        out_specs=jax.tree.map(lambda _: VMEM, out),
        scratch_shapes=list(scratch),
        compiler_params=PARAMS,
        cost_estimate=pl.CostEstimate(flops=flops, bytes_accessed=2**21, transcendentals=0),
    )(*args)


def swap_groups(tiles):
    group = iota((8, 128), 1) >> 4
    for bit in (1, 2, 4):
        low = (group & bit) == 0
        mixed = list(tiles)
        for i in range(8):
            if i & bit == 0:
                j = i | bit
                mixed[i] = jnp.where(low, tiles[i], pltpu.roll(tiles[j], 16 * bit, 1))
                mixed[j] = jnp.where(low, pltpu.roll(tiles[i], 128 - 16 * bit, 1), tiles[j])
        tiles = mixed
    return tiles


def plane_of(kappa, z):
    return jnp.concatenate([kappa[z, pl.ds(c, 8, stride=4), :] for c in range(4)], axis=0)


def beside_xy(plane):
    row, lane = iota((8, 128), 0), iota((GY, 128), 1)
    first, last = plane[0:8], plane[24:32]
    above = jnp.where(row < 7, pltpu.roll(first, 7, 0), 0.0)
    below = jnp.where(row > 0, pltpu.roll(last, 1, 0), 0.0)
    along_y = jnp.concatenate([plane[8:32], above], axis=0) + jnp.concatenate(
        [below, plane[0:24]], axis=0
    )
    right = jnp.where(lane < 127, pltpu.roll(plane, 127, 1), 0.0)
    left = jnp.where(lane > 0, pltpu.roll(plane, 1, 1), 0.0)
    return along_y + right + left


def positions(row):
    target = row >> 8
    member = iota((LANES, CELLS), 0) == target
    order = onehot(iota((CELLS, CELLS), 0) < iota((CELLS, CELLS), 1))
    rank = jnp.where(member, dot(onehot(member), order), 0.0)
    return target, member, jnp.sum(rank, axis=0, keepdims=True).astype(I32)


def slots_of(row):
    target, _, rank = positions(row)
    return iota((SLOTS, CELLS), 0) == target * BOUND + rank


def each(orbitals):
    lane = iota((1, LOCAL), 1)
    return [jnp.max(jnp.where(lane == p, orbitals[...], 0)) for p in range(LOCAL)]


def pack_kernel(first, second, row, down, psi, out):
    target, member, rank = positions(row[...])
    sel = onehot(iota((SLOTS, CELLS), 0) == target * BOUND + rank)
    dens = [
        (psi[a].astype(F32) * psi[b].astype(F32)).astype(BF16)
        for a, b in zip(each(first), each(second))
    ]
    rho = dot_tn(down[...], jnp.concatenate(dens, axis=1)).astype(BF16)
    rho = jnp.concatenate([rho[:, p * CELLS : (p + 1) * CELLS] for p in range(LOCAL)], axis=0)
    sent = dot_nt(sel, rho).astype(BF16)
    for p in range(LOCAL):
        part = sent[:, p * NODES_E : (p + 1) * NODES_E]
        out[:, p * BOUND : (p + 1) * BOUND] = part.reshape(LANES, BOUND, NODES_E)
    number = jnp.where(member, (row[...] & 255) - CELLS, 0).astype(F32).astype(BF16)
    lanes = onehot(iota((NODES_E, CELLS), 0) == rank)
    number = dot_nt(number, lanes) + float(CELLS)
    number = jnp.broadcast_to(number[:, None], (LANES, NUMBERS, NODES_E))
    out[:, LOCAL * BOUND :] = number.astype(BF16)


def placed_bricks(number, arrived, start, count, skip):
    brick = iota((count, SLOTS), 0)
    brick = brick + start + jnp.where(brick >= count // 2, skip, 0)
    parts = [
        arrived[:, p * BOUND : (p + 1) * BOUND].reshape(SLOTS, NODES_E) for p in range(LOCAL)
    ]
    return dot(onehot(brick == number), jnp.concatenate(parts, axis=1))


def two_layers(placed, p, row, diag):
    tiles = swap_groups([placed[p, pl.ds(row + bx, 8, stride=8), :] for bx in range(8)])
    return [
        FOUR_PI * jnp.concatenate(tiles[4 * a : 4 * a + 4], axis=0) / diag[a] for a in range(2)
    ]


def edges_kernel(arrived, kappa, u_out, up_out, down_out, number_out, placed):
    rows = arrived[:, LOCAL * BOUND :].astype(F32).reshape(LANES * NUMBERS, NODES_E).astype(BF16)
    rows = dot(onehot(iota((LANES, rows.shape[0]), 1) == NUMBERS * iota((LANES, rows.shape[0]), 0)), rows)
    rank = onehot(iota((NODES_E, SLOTS), 0) == (iota((NODES_E, SLOTS), 1) & (BOUND - 1)))
    sender = iota((LANES, SLOTS), 0) == (iota((LANES, SLOTS), 1) >> 4)
    number = jnp.where(sender, dot(rows.astype(BF16), rank), 0.0)
    number = jnp.sum(number, axis=0, keepdims=True).astype(I32)
    number_out[...] = number
    wide = placed_bricks(number, arrived, 0, 128, 128)
    for p in range(LOCAL):
        placed[p] = wide[:, p * NODES_E : (p + 1) * NODES_E]
    diag = [6.0 + plane_of(kappa, z) for z in (0, 1, GZ - 2, GZ - 1)]
    for p in range(LOCAL):
        u = two_layers(placed, p, 0, diag[:2]) + two_layers(placed, p, 64, diag[2:])
        for i, plane in enumerate(u):
            u_out[p, i] = plane
        for a in range(2):
            up_out[(p * 2 + a) * GY : (p * 2 + a + 1) * GY] = u[2 + a]
        down_out[p * GY : (p + 1) * GY] = u[0]
    up_out[LOCAL * 2 * GY :] = plane_of(kappa, GZ - 1)


def inner_kernel(first, second, row, number, up, arrived, edges, kappa, pick, spread, orbitals, up_out, u_ref, w_out, sums_out, placed):
    pick[...] = jnp.where(slots_of(row[...]), 1.0, 0.0).T.astype(BF16)
    sel = iota((CELLS, SLOTS), 0) == number[...]
    spread[...] = jnp.where(sel, 1.0, 0.0).T.astype(BF16)
    up_out[...] = up[...]
    lane = iota((META, WIDE), 1)
    numbers = jnp.zeros((META, WIDE), I32)
    for p, (a, b) in enumerate(zip(each(first), each(second))):
        numbers = jnp.where(lane == 2 * p, a, jnp.where(lane == 2 * p + 1, b, numbers))
    orbitals[...] = numbers.astype(F32).astype(BF16)
    diag = [6.0 + plane_of(kappa, z) for z in range(GZ)]
    inverse = [1.0 / d for d in diag]
    wide = placed_bricks(number[...], arrived, 64, 128, 0)
    for p in range(LOCAL):
        placed[p] = wide[:, p * NODES_E : (p + 1) * NODES_E]
    rows = []
    for p in range(LOCAL):
        u = [edges[p, 0], edges[p, 1]]
        u += two_layers(placed, p, 0, diag[2:4]) + two_layers(placed, p, 64, diag[4:6])
        u += [edges[p, 2], edges[p, 3]]
        gamma = delta = eps = cross = jnp.zeros((GY, 128), F32)
        before = jnp.zeros((GY, 128), F32)
        for z in range(GZ):
            centre = u[z]
            u_ref[p, z] = centre
            scaled = diag[z] * centre
            gamma += scaled * centre
            image = scaled - beside_xy(centre)
            if z > 0:
                image = image - u[z - 1]
            if z < GZ - 1:
                image = image - u[z + 1]
            if z in (0, GZ - 1):
                w_out[p, z] = image
                continue
            w = image * inverse[z]
            w_out[p, z] = w
            delta += centre * image
            eps += image * w
            cross += w * (beside_xy(w) + 2.0 * before)
            before = w
        rows += [jnp.sum(v, axis=0, keepdims=True) for v in (gamma, delta, eps, eps - cross)]
    sums_out[...] = jnp.concatenate(rows, axis=0)


def outer_kernel(not_first, not_last, u_ref, w_ref, part, up, down, kappa, ends, sums_out):
    keep, keep_high = not_first[0].astype(F32), not_last[0].astype(F32)
    inverse = [1.0 / (6.0 + k) for k in (up[LOCAL * 2 * GY :], plane_of(kappa, 0), plane_of(kappa, GZ - 1))]
    rows = []
    for p in range(LOCAL):
        far, near = (up[(p * 2 + a) * GY : (p * 2 + a + 1) * GY] for a in range(2))
        low, high = u_ref[p, 0], u_ref[p, GZ - 1]
        w_before = keep * (near - (far + low + beside_xy(near)) * inverse[0])
        q_low = w_ref[p, 0] - keep * near
        q_high = w_ref[p, GZ - 1] - keep_high * down[p * GY : (p + 1) * GY]
        w_low, w_high = q_low * inverse[1], q_high * inverse[2]
        ends[p, 0] = w_low
        ends[p, 1] = w_high
        delta = low * q_low + high * q_high
        eps = q_low * w_low + q_high * w_high
        cross = w_low * (beside_xy(w_low) + 2.0 * (w_before + w_ref[p, 1]))
        cross += w_high * (beside_xy(w_high) + 2.0 * w_ref[p, GZ - 2])
        rows += [jnp.zeros((1, 128), F32)]
        rows += [jnp.sum(v, axis=0, keepdims=True) for v in (delta, eps, eps - cross)]
    sums = jnp.sum(jnp.concatenate(rows, axis=0) + part[...], axis=1, keepdims=True)
    spread = jnp.where(iota((16, 128), 1) == iota((16, 128), 0), sums, 0.0)
    sums_out[...] = jnp.broadcast_to(jnp.sum(spread, axis=0, keepdims=True), (LANES, 128))


def finish_kernel(sums, u_ref, w_ref, ends, spread, potential, out, bricks):
    total = jnp.sum(sums[...], axis=0, keepdims=True)
    lane = iota((1, 128), 1)
    for p in range(LOCAL):
        gamma, delta, eps, zeta = (
            jnp.sum(jnp.where(lane == 4 * p + k, total, 0.0), axis=1, keepdims=True) for k in range(4)
        )
        alpha = gamma / delta
        fresh = alpha * alpha * eps - gamma
        grow = 1.0 + fresh / gamma
        energy = grow * grow * delta - 2.0 * grow * alpha * eps + alpha * alpha * zeta
        later = fresh / energy
        on_u = jnp.broadcast_to(alpha + later * grow, (GY, 128))
        on_w = jnp.broadcast_to(later * alpha, (GY, 128))
        for bz in range(4):
            tiles = []
            for a in range(2):
                z = 2 * bz + a
                w = ends[p, z // (GZ - 1)] if z in (0, GZ - 1) else w_ref[p, z]
                x = on_u * u_ref[p, z] - on_w * w
                for c in range(4):
                    tile = x[8 * c : 8 * c + 8]
                    potential[p, z, pl.ds(c, 8, stride=4), :] = tile
                    tiles.append(tile)
            for bx, tile in enumerate(swap_groups(tiles)):
                bricks[p, pl.ds(bz * 64 + bx, 8, stride=8), :] = tile
    wide = jnp.concatenate([bricks[p].astype(BF16) for p in range(LOCAL)], axis=1)
    out[...] = dot(spread[...], wide).astype(BF16)


def cells_kernel(pick, returned, orbitals, out):
    out[:CELLS] = dot(pick[...], returned[...]).astype(BF16)
    out[CELLS:] = orbitals[...]


def terms_kernel(count, started, *refs):
    wanted, (up, psi, block, *totals) = refs[:count], refs[count:]
    if started:
        earlier, totals = totals[:count], totals[count:]
    orbitals = block[CELLS:, :128].astype(F32).astype(I32)
    lane = iota((META, 128), 1)
    read = [jnp.max(jnp.where(lane == k, orbitals, 0)) for k in range(2 * LOCAL)]
    for k, total in enumerate(totals):
        total[...] = earlier[k][...] if started else jnp.zeros_like(total)
    for p in range(LOCAL):
        for k, total in enumerate(totals):

            @pl.when(read[2 * p] == wanted[k][0])
            def _():
                orbital = psi[read[2 * p + 1]].astype(F32)
                cellv = block[:CELLS, p * 128 : (p + 1) * 128]
                total[...] += dot_nt(up[...], cellv) * orbital


def add_terms(block, wanted, up, psi, earlier):
    total = jax.ShapeDtypeStruct((NODES_W, CELLS), F32)
    count = len(wanted)
    return call(
        functools.partial(terms_kernel, count, bool(earlier)),
        (total,) * count,
        [SMEM] * count + [VMEM] * (3 + len(earlier)),
        (*wanted, up, psi, block, *earlier),
    )


def join_kernel(own, given, out):
    total = own[...] + given[...]
    out[:, 0, :] = total[:, :128]
    out[:, 1, :] = total[:, 128:]


def on_device(psi, kappa, interp_down, interp_up, brick_of_cell, pair_first, pair_second):
    struct = jax.ShapeDtypeStruct
    field = struct((LOCAL, GZ, GY, GX), F32)
    row = brick_of_cell.reshape(1, CELLS)
    first, second = pair_first.reshape(1, LOCAL), pair_second.reshape(1, LOCAL)
    out = call(
        pack_kernel,
        struct((LANES, LOCAL * BOUND + NUMBERS, NODES_E), BF16),
        [VMEM] * 5,
        (first, second, row, interp_down.T, psi),
    )
    arrived = lax.all_to_all(out, "mesh", 0, 0, tiled=True)
    half = pltpu.VMEM((LOCAL, CELLS // 2, NODES_E), F32)
    edges, up, down, number = call(
        edges_kernel,
        (
            struct((LOCAL, 4, GY, GX), F32),
            struct(((LOCAL * 2 + 1) * GY, GX), F32),
            struct((LOCAL * GY, GX), F32),
            struct((1, SLOTS), I32),
        ),
        [VMEM, VMEM],
        (arrived, kappa),
        [half],
    )
    up = lax.ppermute(up, "mesh", [(i, (i + 1) % LANES) for i in range(LANES)])
    down = lax.ppermute(down, "mesh", [((i + 1) % LANES, i) for i in range(LANES)])
    place = lax.axis_index("mesh")
    not_first, not_last = (
        inside.astype(I32).reshape(1) for inside in (place > 0, place < LANES - 1)
    )
    pick, spread, orbitals, upward, u, w, part = call(
        inner_kernel,
        (
            struct((CELLS, SLOTS), BF16),
            struct((SLOTS, CELLS), BF16),
            struct((META, WIDE), BF16),
            struct((NODES_W, NODES_E), BF16),
            field,
            field,
            struct((16, 128), F32),
        ),
        [VMEM] * 8,
        (first, second, row, number, interp_up, arrived, edges, kappa),
        [half],
    )
    ends, sums = call(
        outer_kernel,
        (struct((LOCAL, 2, GY, GX), F32), struct((LANES, 128), F32)),
        [SMEM] * 2 + [VMEM] * 6,
        (not_first, not_last, u, w, part, up, down, kappa),
    )
    sums = lax.all_to_all(sums, "mesh", 0, 0, tiled=True)
    potential, back = call(
        finish_kernel,
        (field, struct((SLOTS, WIDE), BF16)),
        [VMEM, VMEM, VMEM, VMEM, VMEM],
        (sums, u, w, ends, spread),
        [pltpu.VMEM((LOCAL, CELLS, NODES_E), F32)],
    )
    returned = lax.all_to_all(back, "mesh", 0, 0, tiled=True)
    value = call(
        cells_kernel,
        struct((CELLS + META, WIDE), BF16),
        [VMEM] * 3,
        (pick, returned, orbitals),
    )

    def along_x(value, by):
        return lax.ppermute(value, "pair", [(i, (i + by) % ORB) for i in range(ORB)])

    right, left, across = (along_x(value, by) for by in (2, -2, 4))
    me = lax.axis_index("pair").astype(I32)
    mine, others = me.reshape(1), (me ^ 1).reshape(1)
    parts = ()
    for block in (value, left, across):
        parts = add_terms(block, (mine, others), upward, psi, parts)
    own, other = parts
    (other,) = add_terms(right, (others,), upward, psi, (other,))
    given = lax.ppermute(other, "pair", [(i, i ^ 1) for i in range(ORB)])
    (own,) = add_terms(right, (mine,), upward, psi, (own,))
    action = call(
        join_kernel, struct((NODES_W, 2, CELLS // 2), F32), [VMEM, VMEM], (own, given)
    )
    return potential, action.reshape(1, NODES_W, CELLS)


def solution(mesh):
    return jax.shard_map(
        on_device,
        mesh=mesh,
        in_specs=(
            P(None, None, "mesh"),
            P("mesh", None, None),
            P(),
            P(),
            P("mesh"),
            P("pair"),
            P("pair"),
        ),
        out_specs=(P("pair", "mesh", None, None), P("pair", None, "mesh")),
        check_vma=False,
    )
```

```python
import functools
import math

import jax
import jax.numpy as jnp
from jax import lax
from jax.experimental import pallas as pl
from jax.experimental.pallas import tpu as pltpu
from jax.sharding import PartitionSpec as P

F32 = jnp.float32
BF16 = jnp.bfloat16
I32 = jnp.int32
FOUR_PI = 4.0 * math.pi

LANES = 32
BOUND = 16
CELLS = 256
SLOTS = LANES * BOUND
NODES_W = 343
NODES_E = 128
LOCAL = 4
ORB = 8
GZ, GY, GX = 8, 32, 128
WIDE = LOCAL * NODES_E
NUMBERS = 8
META = 8

VMEM = pl.BlockSpec(memory_space=pltpu.VMEM)
SMEM = pl.BlockSpec(memory_space=pltpu.SMEM)
PARAMS = pltpu.CompilerParams(vmem_limit_bytes=16 * 1024 * 1024)


def iota(shape, dim):
    return lax.broadcasted_iota(I32, shape, dim)


def onehot(condition):
    return jnp.where(condition, 1.0, 0.0).astype(BF16)


def dot(left, right):
    return lax.dot_general(left, right, (((1,), (0,)), ((), ())), preferred_element_type=F32)


def dot_nt(left, right):
    return lax.dot_general(left, right, (((1,), (1,)), ((), ())), preferred_element_type=F32)


def dot_tn(left, right):
    return lax.dot_general(left, right, (((0,), (0,)), ((), ())), preferred_element_type=F32)


def call(body, out, specs, args, scratch=(), flops=10**7):
    return pl.pallas_call(
        body,
        out_shape=out,
        in_specs=specs,
        out_specs=jax.tree.map(lambda _: VMEM, out),
        scratch_shapes=list(scratch),
        compiler_params=PARAMS,
        cost_estimate=pl.CostEstimate(flops=flops, bytes_accessed=2**21, transcendentals=0),
    )(*args)


def swap_groups(tiles):
    group = iota((8, 128), 1) >> 4
    for bit in (1, 2, 4):
        low = (group & bit) == 0
        mixed = list(tiles)
        for i in range(8):
            if i & bit == 0:
                j = i | bit
                mixed[i] = jnp.where(low, tiles[i], pltpu.roll(tiles[j], 16 * bit, 1))
                mixed[j] = jnp.where(low, pltpu.roll(tiles[i], 128 - 16 * bit, 1), tiles[j])
        tiles = mixed
    return tiles


def plane_of(kappa, z):
    return jnp.concatenate([kappa[z, pl.ds(c, 8, stride=4), :] for c in range(4)], axis=0)


def beside_xy(plane):
    row, lane = iota((8, 128), 0), iota((GY, 128), 1)
    first, last = plane[0:8], plane[24:32]
    above = jnp.where(row < 7, pltpu.roll(first, 7, 0), 0.0)
    below = jnp.where(row > 0, pltpu.roll(last, 1, 0), 0.0)
    along_y = jnp.concatenate([plane[8:32], above], axis=0) + jnp.concatenate(
        [below, plane[0:24]], axis=0
    )
    right = jnp.where(lane < 127, pltpu.roll(plane, 127, 1), 0.0)
    left = jnp.where(lane > 0, pltpu.roll(plane, 1, 1), 0.0)
    return along_y + right + left


def positions(row):
    target = row >> 8
    member = iota((LANES, CELLS), 0) == target
    order = onehot(iota((CELLS, CELLS), 0) < iota((CELLS, CELLS), 1))
    rank = jnp.where(member, dot(onehot(member), order), 0.0)
    return target, member, jnp.sum(rank, axis=0, keepdims=True).astype(I32)


def slots_of(row):
    target, _, rank = positions(row)
    return iota((SLOTS, CELLS), 0) == target * BOUND + rank


def each(orbitals):
    lane = iota((1, LOCAL), 1)
    return [jnp.max(jnp.where(lane == p, orbitals[...], 0)) for p in range(LOCAL)]


def pack_kernel(here, first, second, row, down, psi, out):
    target, member, rank = positions(row[...])
    sel = onehot(iota((SLOTS, CELLS), 0) == target * BOUND + rank)
    dens = [
        (psi[a].astype(F32) * psi[b].astype(F32)).astype(BF16)
        for a, b in zip(each(first), each(second))
    ]
    rho = dot_tn(down[...], jnp.concatenate(dens, axis=1)).astype(BF16)
    rho = jnp.concatenate([rho[:, p * CELLS : (p + 1) * CELLS] for p in range(LOCAL)], axis=0)
    sent = dot_nt(sel, rho).astype(BF16)
    for p in range(LOCAL):
        part = sent[:, p * NODES_E : (p + 1) * NODES_E]
        out[:, p * BOUND : (p + 1) * BOUND] = part.reshape(LANES, BOUND, NODES_E)
    number = jnp.where(member, (row[...] & 255) + 1, 0).astype(F32).astype(BF16)
    lanes = onehot(iota((NODES_E, CELLS), 0) == rank + BOUND * (here[0] & (NUMBERS - 1)))
    number = jnp.broadcast_to(dot_nt(number, lanes)[:, None], (LANES, NUMBERS, NODES_E))
    out[:, LOCAL * BOUND :] = number.astype(BF16)


def placed_bricks(number, arrived, start, count, skip):
    brick = iota((count, SLOTS), 0)
    brick = brick + start + jnp.where(brick >= count // 2, skip, 0)
    parts = [
        arrived[:, p * BOUND : (p + 1) * BOUND].reshape(SLOTS, NODES_E) for p in range(LOCAL)
    ]
    return dot(onehot(brick == number), jnp.concatenate(parts, axis=1))


def two_layers(placed, p, row, diag):
    tiles = swap_groups([placed[p, pl.ds(row + bx, 8, stride=8), :] for bx in range(8)])
    return [
        FOUR_PI * jnp.concatenate(tiles[4 * a : 4 * a + 4], axis=0) / diag[a] for a in range(2)
    ]


def edges_kernel(arrived, kappa, u_out, up_out, down_out, number_out, placed):
    rows = arrived[:, LOCAL * BOUND :].astype(F32).reshape(4, LANES // 4 * NUMBERS, NODES_E)
    rows = jnp.sum(rows, axis=1, keepdims=True) * (1.0 / NUMBERS)
    number = jnp.concatenate([rows[i] for i in range(4)], axis=1).astype(I32) - 1
    number_out[...] = number
    wide = placed_bricks(number, arrived, 0, 128, 128)
    for p in range(LOCAL):
        placed[p] = wide[:, p * NODES_E : (p + 1) * NODES_E]
    diag = [6.0 + plane_of(kappa, z) for z in (0, 1, GZ - 2, GZ - 1)]
    for p in range(LOCAL):
        u = two_layers(placed, p, 0, diag[:2]) + two_layers(placed, p, 64, diag[2:])
        for i, plane in enumerate(u):
            u_out[p, i] = plane
        for a in range(2):
            up_out[(p * 2 + a) * GY : (p * 2 + a + 1) * GY] = u[2 + a]
        down_out[p * GY : (p + 1) * GY] = u[0]
    up_out[LOCAL * 2 * GY :] = plane_of(kappa, GZ - 1)


def inner_kernel(first, second, row, number, up, arrived, edges, kappa, pick, spread, orbitals, up_out, u_ref, w_out, sums_out, placed):
    pick[...] = jnp.where(slots_of(row[...]), 1.0, 0.0).T.astype(BF16)
    sel = iota((CELLS, SLOTS), 0) == number[...]
    spread[...] = jnp.where(sel, 1.0, 0.0).T.astype(BF16)
    up_out[...] = up[...]
    lane = iota((META, WIDE), 1)
    numbers = jnp.zeros((META, WIDE), I32)
    for p, (a, b) in enumerate(zip(each(first), each(second))):
        numbers = jnp.where(lane == 2 * p, a, jnp.where(lane == 2 * p + 1, b, numbers))
    orbitals[...] = numbers.astype(F32).astype(BF16)
    diag = [6.0 + plane_of(kappa, z) for z in range(GZ)]
    inverse = [1.0 / d for d in diag]
    wide = placed_bricks(number[...], arrived, 64, 128, 0)
    for p in range(LOCAL):
        placed[p] = wide[:, p * NODES_E : (p + 1) * NODES_E]
    rows = []
    for p in range(LOCAL):
        u = [edges[p, 0], edges[p, 1]]
        u += two_layers(placed, p, 0, diag[2:4]) + two_layers(placed, p, 64, diag[4:6])
        u += [edges[p, 2], edges[p, 3]]
        gamma = delta = eps = cross = jnp.zeros((GY, 128), F32)
        before = jnp.zeros((GY, 128), F32)
        for z in range(GZ):
            centre = u[z]
            u_ref[p, z] = centre
            scaled = diag[z] * centre
            gamma += scaled * centre
            image = scaled - beside_xy(centre)
            if z > 0:
                image = image - u[z - 1]
            if z < GZ - 1:
                image = image - u[z + 1]
            if z in (0, GZ - 1):
                w_out[p, z] = image
                continue
            w = image * inverse[z]
            w_out[p, z] = w
            delta += centre * image
            eps += image * w
            cross += w * (beside_xy(w) + 2.0 * before)
            before = w
        rows += [jnp.sum(v, axis=0, keepdims=True) for v in (gamma, delta, eps, eps - cross)]
    sums_out[...] = jnp.concatenate(rows, axis=0)


def outer_kernel(not_first, not_last, u_ref, w_ref, part, up, down, kappa, ends, sums_out):
    keep, keep_high = not_first[0].astype(F32), not_last[0].astype(F32)
    inverse = [1.0 / (6.0 + k) for k in (up[LOCAL * 2 * GY :], plane_of(kappa, 0), plane_of(kappa, GZ - 1))]
    rows = []
    for p in range(LOCAL):
        far, near = (up[(p * 2 + a) * GY : (p * 2 + a + 1) * GY] for a in range(2))
        low, high = u_ref[p, 0], u_ref[p, GZ - 1]
        w_before = keep * (near - (far + low + beside_xy(near)) * inverse[0])
        q_low = w_ref[p, 0] - keep * near
        q_high = w_ref[p, GZ - 1] - keep_high * down[p * GY : (p + 1) * GY]
        w_low, w_high = q_low * inverse[1], q_high * inverse[2]
        ends[p, 0] = w_low
        ends[p, 1] = w_high
        delta = low * q_low + high * q_high
        eps = q_low * w_low + q_high * w_high
        cross = w_low * (beside_xy(w_low) + 2.0 * (w_before + w_ref[p, 1]))
        cross += w_high * (beside_xy(w_high) + 2.0 * w_ref[p, GZ - 2])
        rows += [jnp.zeros((1, 128), F32)]
        rows += [jnp.sum(v, axis=0, keepdims=True) for v in (delta, eps, eps - cross)]
    sums = jnp.sum(jnp.concatenate(rows, axis=0) + part[...], axis=1, keepdims=True)
    spread = jnp.where(iota((16, 128), 1) == iota((16, 128), 0), sums, 0.0)
    sums_out[...] = jnp.broadcast_to(jnp.sum(spread, axis=0, keepdims=True), (LANES, 128))


def finish_kernel(sums, u_ref, w_ref, ends, spread, potential, out, bricks):
    total = jnp.sum(sums[...], axis=0, keepdims=True)
    lane = iota((1, 128), 1)
    for p in range(LOCAL):
        gamma, delta, eps, zeta = (
            jnp.sum(jnp.where(lane == 4 * p + k, total, 0.0), axis=1, keepdims=True) for k in range(4)
        )
        alpha = gamma / delta
        fresh = alpha * alpha * eps - gamma
        grow = 1.0 + fresh / gamma
        energy = grow * grow * delta - 2.0 * grow * alpha * eps + alpha * alpha * zeta
        later = fresh / energy
        on_u = jnp.broadcast_to(alpha + later * grow, (GY, 128))
        on_w = jnp.broadcast_to(later * alpha, (GY, 128))
        for bz in range(4):
            tiles = []
            for a in range(2):
                z = 2 * bz + a
                w = ends[p, z // (GZ - 1)] if z in (0, GZ - 1) else w_ref[p, z]
                x = on_u * u_ref[p, z] - on_w * w
                for c in range(4):
                    tile = x[8 * c : 8 * c + 8]
                    potential[p, z, pl.ds(c, 8, stride=4), :] = tile
                    tiles.append(tile)
            for bx, tile in enumerate(swap_groups(tiles)):
                bricks[p, pl.ds(bz * 64 + bx, 8, stride=8), :] = tile
    wide = jnp.concatenate([bricks[p].astype(BF16) for p in range(LOCAL)], axis=1)
    out[...] = dot(spread[...], wide).astype(BF16)


def cells_kernel(pick, returned, orbitals, out):
    out[:CELLS] = dot(pick[...], returned[...]).astype(BF16)
    out[CELLS:] = orbitals[...]


def terms_kernel(count, started, *refs):
    wanted, (up, psi, block, *totals) = refs[:count], refs[count:]
    if started:
        earlier, totals = totals[:count], totals[count:]
    orbitals = block[CELLS:, :128].astype(F32).astype(I32)
    lane = iota((META, 128), 1)
    read = [jnp.max(jnp.where(lane == k, orbitals, 0)) for k in range(2 * LOCAL)]
    for k, total in enumerate(totals):
        total[...] = earlier[k][...] if started else jnp.zeros_like(total)
    for p in range(LOCAL):
        for k, total in enumerate(totals):

            @pl.when(read[2 * p] == wanted[k][0])
            def _():
                orbital = psi[read[2 * p + 1]].astype(F32)
                cellv = block[:CELLS, p * 128 : (p + 1) * 128]
                total[...] += dot_nt(up[...], cellv) * orbital


def add_terms(block, wanted, up, psi, earlier):
    total = jax.ShapeDtypeStruct((NODES_W, CELLS), F32)
    count = len(wanted)
    return call(
        functools.partial(terms_kernel, count, bool(earlier)),
        (total,) * count,
        [SMEM] * count + [VMEM] * (3 + len(earlier)),
        (*wanted, up, psi, block, *earlier),
    )


def join_kernel(own, given, out):
    out[:, 0, :] = own[...] + given[...]


def on_device(psi, kappa, interp_down, interp_up, brick_of_cell, pair_first, pair_second):
    struct = jax.ShapeDtypeStruct
    field = struct((LOCAL, GZ, GY, GX), F32)
    place = lax.axis_index("mesh")
    row = brick_of_cell.reshape(1, CELLS)
    first, second = pair_first.reshape(1, LOCAL), pair_second.reshape(1, LOCAL)
    out = call(
        pack_kernel,
        struct((LANES, LOCAL * BOUND + NUMBERS, NODES_E), BF16),
        [SMEM] + [VMEM] * 5,
        (place.astype(I32).reshape(1), first, second, row, interp_down.T, psi),
    )
    arrived = lax.all_to_all(out, "mesh", 0, 0, tiled=True)
    half = pltpu.VMEM((LOCAL, CELLS // 2, NODES_E), F32)
    edges, up, down, number = call(
        edges_kernel,
        (
            struct((LOCAL, 4, GY, GX), F32),
            struct(((LOCAL * 2 + 1) * GY, GX), F32),
            struct((LOCAL * GY, GX), F32),
            struct((1, SLOTS), I32),
        ),
        [VMEM, VMEM],
        (arrived, kappa),
        [half],
    )
    up = lax.ppermute(up, "mesh", [(i, (i + 1) % LANES) for i in range(LANES)])
    down = lax.ppermute(down, "mesh", [((i + 1) % LANES, i) for i in range(LANES)])
    not_first, not_last = (
        inside.astype(I32).reshape(1) for inside in (place > 0, place < LANES - 1)
    )
    pick, spread, orbitals, upward, u, w, part = call(
        inner_kernel,
        (
            struct((CELLS, SLOTS), BF16),
            struct((SLOTS, CELLS), BF16),
            struct((META, WIDE), BF16),
            struct((NODES_W, NODES_E), BF16),
            field,
            field,
            struct((16, 128), F32),
        ),
        [VMEM] * 8,
        (first, second, row, number, interp_up, arrived, edges, kappa),
        [half],
    )
    ends, sums = call(
        outer_kernel,
        (struct((LOCAL, 2, GY, GX), F32), struct((LANES, 128), F32)),
        [SMEM] * 2 + [VMEM] * 6,
        (not_first, not_last, u, w, part, up, down, kappa),
    )
    sums = lax.all_to_all(sums, "mesh", 0, 0, tiled=True)
    potential, back = call(
        finish_kernel,
        (field, struct((SLOTS, WIDE), BF16)),
        [VMEM, VMEM, VMEM, VMEM, VMEM],
        (sums, u, w, ends, spread),
        [pltpu.VMEM((LOCAL, CELLS, NODES_E), F32)],
    )
    returned = lax.all_to_all(back, "mesh", 0, 0, tiled=True)
    value = call(
        cells_kernel,
        struct((CELLS + META, WIDE), BF16),
        [VMEM] * 3,
        (pick, returned, orbitals),
    )

    def along_x(value, by):
        return lax.ppermute(value, "pair", [(i, (i + by) % ORB) for i in range(ORB)])

    right, left, across = (along_x(value, by) for by in (2, -2, 4))
    me = lax.axis_index("pair").astype(I32)
    mine, others = me.reshape(1), (me ^ 1).reshape(1)
    parts = ()
    for block in (value, left, across):
        parts = add_terms(block, (mine, others), upward, psi, parts)
    own, other = parts
    (other,) = add_terms(right, (others,), upward, psi, (other,))
    given = lax.ppermute(other, "pair", [(i, i ^ 1) for i in range(ORB)])
    (own,) = add_terms(right, (mine,), upward, psi, (own,))
    action = call(
        join_kernel, struct((NODES_W, 1, CELLS), F32), [VMEM, VMEM], (own, given)
    )
    return potential, action.reshape(1, NODES_W, CELLS)


def solution(mesh):
    return jax.shard_map(
        on_device,
        mesh=mesh,
        in_specs=(
            P(None, None, "mesh"),
            P("mesh", None, None),
            P(),
            P(),
            P("mesh"),
            P("pair"),
            P("pair"),
        ),
        out_specs=(P("pair", "mesh", None, None), P("pair", None, "mesh")),
        check_vma=False,
    )
```

```python
import functools
import math

import jax
import jax.numpy as jnp
from jax import lax
from jax.experimental import pallas as pl
from jax.experimental.pallas import tpu as pltpu
from jax.sharding import PartitionSpec as P

F32 = jnp.float32
BF16 = jnp.bfloat16
I32 = jnp.int32
FOUR_PI = 4.0 * math.pi

LANES = 32
BOUND = 16
CELLS = 256
SLOTS = LANES * BOUND
NODES_W = 343
NODES_E = 128
LOCAL = 4
ORB = 8
GZ, GY, GX = 8, 32, 128
WIDE = LOCAL * NODES_E
NUMBERS = 8
META = 8

VMEM = pl.BlockSpec(memory_space=pltpu.VMEM)
SMEM = pl.BlockSpec(memory_space=pltpu.SMEM)
PARAMS = pltpu.CompilerParams(vmem_limit_bytes=16 * 1024 * 1024)


def iota(shape, dim):
    return lax.broadcasted_iota(I32, shape, dim)


def onehot(condition):
    return jnp.where(condition, 1.0, 0.0).astype(BF16)


def dot(left, right):
    return lax.dot_general(left, right, (((1,), (0,)), ((), ())), preferred_element_type=F32)


def dot_nt(left, right):
    return lax.dot_general(left, right, (((1,), (1,)), ((), ())), preferred_element_type=F32)


def dot_tn(left, right):
    return lax.dot_general(left, right, (((0,), (0,)), ((), ())), preferred_element_type=F32)


def call(body, out, specs, args, scratch=(), flops=10**7):
    return pl.pallas_call(
        body,
        out_shape=out,
        in_specs=specs,
        out_specs=jax.tree.map(lambda _: VMEM, out),
        scratch_shapes=list(scratch),
        compiler_params=PARAMS,
        cost_estimate=pl.CostEstimate(flops=flops, bytes_accessed=2**21, transcendentals=0),
    )(*args)


def swap_groups(tiles):
    group = iota((8, 128), 1) >> 4
    for bit in (1, 2, 4):
        low = (group & bit) == 0
        mixed = list(tiles)
        for i in range(8):
            if i & bit == 0:
                j = i | bit
                mixed[i] = jnp.where(low, tiles[i], pltpu.roll(tiles[j], 16 * bit, 1))
                mixed[j] = jnp.where(low, pltpu.roll(tiles[i], 128 - 16 * bit, 1), tiles[j])
        tiles = mixed
    return tiles


def plane_of(kappa, z):
    return jnp.concatenate([kappa[z, pl.ds(c, 8, stride=4), :] for c in range(4)], axis=0)


def beside_xy(plane):
    row, lane = iota((8, 128), 0), iota((GY, 128), 1)
    first, last = plane[0:8], plane[24:32]
    above = jnp.where(row < 7, pltpu.roll(first, 7, 0), 0.0)
    below = jnp.where(row > 0, pltpu.roll(last, 1, 0), 0.0)
    along_y = jnp.concatenate([plane[8:32], above], axis=0) + jnp.concatenate(
        [below, plane[0:24]], axis=0
    )
    right = jnp.where(lane < 127, pltpu.roll(plane, 127, 1), 0.0)
    left = jnp.where(lane > 0, pltpu.roll(plane, 1, 1), 0.0)
    return along_y + right + left


def positions(row):
    target = row >> 8
    member = iota((LANES, CELLS), 0) == target
    order = onehot(iota((CELLS, CELLS), 0) < iota((CELLS, CELLS), 1))
    rank = jnp.where(member, dot(onehot(member), order), 0.0)
    return target, member, jnp.sum(rank, axis=0, keepdims=True).astype(I32)


def slots_of(row):
    target, _, rank = positions(row)
    return iota((SLOTS, CELLS), 0) == target * BOUND + rank


def each(orbitals):
    lane = iota((1, LOCAL), 1)
    return [jnp.max(jnp.where(lane == p, orbitals[...], 0)) for p in range(LOCAL)]


def pack_kernel(here, first, second, row, down, psi, out):
    target, member, rank = positions(row[...])
    sel = onehot(iota((SLOTS, CELLS), 0) == target * BOUND + rank)
    dens = [
        (psi[a].astype(F32) * psi[b].astype(F32)).astype(BF16)
        for a, b in zip(each(first), each(second))
    ]
    rho = dot_tn(down[...], jnp.concatenate(dens, axis=1)).astype(BF16)
    rho = jnp.concatenate([rho[:, p * CELLS : (p + 1) * CELLS] for p in range(LOCAL)], axis=0)
    sent = dot_nt(sel, rho).astype(BF16)
    for p in range(LOCAL):
        part = sent[:, p * NODES_E : (p + 1) * NODES_E]
        out[:, p * BOUND : (p + 1) * BOUND] = part.reshape(LANES, BOUND, NODES_E)
    number = jnp.where(member, (row[...] & 255) + 1, 0).astype(F32).astype(BF16)
    lanes = onehot(iota((NODES_E, CELLS), 0) == rank + BOUND * (here[0] & (NUMBERS - 1)))
    number = jnp.broadcast_to(dot_nt(number, lanes)[:, None], (LANES, NUMBERS, NODES_E))
    out[:, LOCAL * BOUND :] = number.astype(BF16)


def placed_bricks(number, arrived, start, count, skip):
    brick = iota((count, SLOTS), 0)
    brick = brick + start + jnp.where(brick >= count // 2, skip, 0)
    parts = [
        arrived[:, p * BOUND : (p + 1) * BOUND].reshape(SLOTS, NODES_E) for p in range(LOCAL)
    ]
    return dot(onehot(brick == number), jnp.concatenate(parts, axis=1))


def two_layers(placed, p, row, diag):
    tiles = swap_groups([placed[p, pl.ds(row + bx, 8, stride=8), :] for bx in range(8)])
    return [
        FOUR_PI * jnp.concatenate(tiles[4 * a : 4 * a + 4], axis=0) / diag[a] for a in range(2)
    ]


def edges_kernel(arrived, kappa, u_out, up_out, down_out, number_out, placed):
    rows = arrived[:, LOCAL * BOUND :].astype(F32).reshape(4, LANES // 4 * NUMBERS, NODES_E)
    rows = jnp.sum(rows, axis=1, keepdims=True) * (1.0 / NUMBERS)
    number = jnp.concatenate([rows[i] for i in range(4)], axis=1).astype(I32) - 1
    number_out[...] = number
    wide = placed_bricks(number, arrived, 0, 128, 128)
    for p in range(LOCAL):
        placed[p] = wide[:, p * NODES_E : (p + 1) * NODES_E]
    diag = [6.0 + plane_of(kappa, z) for z in (0, 1, GZ - 2, GZ - 1)]
    for p in range(LOCAL):
        u = two_layers(placed, p, 0, diag[:2]) + two_layers(placed, p, 64, diag[2:])
        for i, plane in enumerate(u):
            u_out[p, i] = plane
        for a in range(2):
            up_out[(p * 2 + a) * GY : (p * 2 + a + 1) * GY] = u[2 + a]
        down_out[p * GY : (p + 1) * GY] = u[0]
    up_out[LOCAL * 2 * GY :] = plane_of(kappa, GZ - 1)


def inner_kernel(first, second, row, number, up, arrived, edges, kappa, pick, spread, orbitals, up_out, u_ref, w_out, sums_out, placed):
    pick[...] = jnp.where(slots_of(row[...]), 1.0, 0.0).T.astype(BF16)
    sel = iota((CELLS, SLOTS), 0) == number[...]
    spread[...] = jnp.where(sel, 1.0, 0.0).T.astype(BF16)
    up_out[...] = up[...]
    lane = iota((META, WIDE), 1)
    numbers = jnp.zeros((META, WIDE), I32)
    for p, (a, b) in enumerate(zip(each(first), each(second))):
        numbers = jnp.where(lane == 2 * p, a, jnp.where(lane == 2 * p + 1, b, numbers))
    orbitals[...] = numbers.astype(F32).astype(BF16)
    diag = [6.0 + plane_of(kappa, z) for z in range(GZ)]
    inverse = [1.0 / d for d in diag]
    wide = placed_bricks(number[...], arrived, 64, 128, 0)
    for p in range(LOCAL):
        placed[p] = wide[:, p * NODES_E : (p + 1) * NODES_E]
    rows = []
    for p in range(LOCAL):
        u = [edges[p, 0], edges[p, 1]]
        u += two_layers(placed, p, 0, diag[2:4]) + two_layers(placed, p, 64, diag[4:6])
        u += [edges[p, 2], edges[p, 3]]
        gamma = delta = eps = cross = jnp.zeros((GY, 128), F32)
        before = jnp.zeros((GY, 128), F32)
        for z in range(GZ):
            centre = u[z]
            u_ref[p, z] = centre
            scaled = diag[z] * centre
            gamma += scaled * centre
            image = scaled - beside_xy(centre)
            if z > 0:
                image = image - u[z - 1]
            if z < GZ - 1:
                image = image - u[z + 1]
            if z in (0, GZ - 1):
                w_out[p, z] = image
                continue
            w = image * inverse[z]
            w_out[p, z] = w
            delta += centre * image
            eps += image * w
            cross += w * (beside_xy(w) + 2.0 * before)
            before = w
        rows += [jnp.sum(v, axis=0, keepdims=True) for v in (gamma, delta, eps, eps - cross)]
    sums_out[...] = jnp.concatenate(rows, axis=0)


def outer_kernel(not_first, not_last, u_ref, w_ref, part, up, down, kappa, ends, sums_out):
    keep, keep_high = not_first[0].astype(F32), not_last[0].astype(F32)
    inverse = [1.0 / (6.0 + k) for k in (up[LOCAL * 2 * GY :], plane_of(kappa, 0), plane_of(kappa, GZ - 1))]
    rows = []
    for p in range(LOCAL):
        far, near = (up[(p * 2 + a) * GY : (p * 2 + a + 1) * GY] for a in range(2))
        low, high = u_ref[p, 0], u_ref[p, GZ - 1]
        w_before = keep * (near - (far + low + beside_xy(near)) * inverse[0])
        q_low = w_ref[p, 0] - keep * near
        q_high = w_ref[p, GZ - 1] - keep_high * down[p * GY : (p + 1) * GY]
        w_low, w_high = q_low * inverse[1], q_high * inverse[2]
        ends[p, 0] = w_low
        ends[p, 1] = w_high
        delta = low * q_low + high * q_high
        eps = q_low * w_low + q_high * w_high
        cross = w_low * (beside_xy(w_low) + 2.0 * (w_before + w_ref[p, 1]))
        cross += w_high * (beside_xy(w_high) + 2.0 * w_ref[p, GZ - 2])
        rows += [jnp.zeros((1, 128), F32)]
        rows += [jnp.sum(v, axis=0, keepdims=True) for v in (delta, eps, eps - cross)]
    sums = jnp.sum(jnp.concatenate(rows, axis=0) + part[...], axis=1, keepdims=True)
    spread = jnp.where(iota((16, 128), 1) == iota((16, 128), 0), sums, 0.0)
    sums_out[...] = jnp.broadcast_to(jnp.sum(spread, axis=0, keepdims=True), (LANES, 128))


def finish_kernel(sums, u_ref, w_ref, ends, spread, potential, out, bricks):
    total = jnp.sum(sums[...], axis=0, keepdims=True)
    lane = iota((1, 128), 1)
    for p in range(LOCAL):
        gamma, delta, eps, zeta = (
            jnp.sum(jnp.where(lane == 4 * p + k, total, 0.0), axis=1, keepdims=True) for k in range(4)
        )
        alpha = gamma / delta
        fresh = alpha * alpha * eps - gamma
        grow = 1.0 + fresh / gamma
        energy = grow * grow * delta - 2.0 * grow * alpha * eps + alpha * alpha * zeta
        later = fresh / energy
        on_u = jnp.broadcast_to(alpha + later * grow, (GY, 128))
        on_w = jnp.broadcast_to(later * alpha, (GY, 128))
        for bz in range(4):
            tiles = []
            for a in range(2):
                z = 2 * bz + a
                w = ends[p, z // (GZ - 1)] if z in (0, GZ - 1) else w_ref[p, z]
                x = on_u * u_ref[p, z] - on_w * w
                for c in range(4):
                    tile = x[8 * c : 8 * c + 8]
                    potential[p, z, pl.ds(c, 8, stride=4), :] = tile
                    tiles.append(tile)
            for bx, tile in enumerate(swap_groups(tiles)):
                bricks[p, pl.ds(bz * 64 + bx, 8, stride=8), :] = tile
    wide = jnp.concatenate([bricks[p].astype(BF16) for p in range(LOCAL)], axis=1)
    out[...] = dot(spread[...], wide).astype(BF16)


def cells_kernel(pick, returned, orbitals, out):
    out[:CELLS] = dot(pick[...], returned[...]).astype(BF16)
    out[CELLS:] = orbitals[...]


def terms_kernel(count, started, *refs):
    wanted, (up, psi, block, *totals) = refs[:count], refs[count:]
    if started:
        earlier, totals = totals[:count], totals[count:]
    orbitals = block[CELLS:, :128].astype(F32).astype(I32)
    lane = iota((META, 128), 1)
    read = [jnp.max(jnp.where(lane == k, orbitals, 0)) for k in range(2 * LOCAL)]
    for k, total in enumerate(totals):
        total[...] = earlier[k][...] if started else jnp.zeros_like(total)
    for p in range(LOCAL):
        for k, total in enumerate(totals):

            @pl.when(read[2 * p] == wanted[k][0])
            def _():
                orbital = psi[read[2 * p + 1]].astype(F32)
                cellv = block[:CELLS, p * 128 : (p + 1) * 128]
                total[...] += dot_nt(up[...], cellv) * orbital


def add_terms(block, wanted, up, psi, earlier):
    total = jax.ShapeDtypeStruct((NODES_W, CELLS), F32)
    count = len(wanted)
    return call(
        functools.partial(terms_kernel, count, bool(earlier)),
        (total,) * count,
        [SMEM] * count + [VMEM] * (3 + len(earlier)),
        (*wanted, up, psi, block, *earlier),
    )


def join_kernel(own, given, out):
    out[:, 0, :] = own[...] + given[...]


def on_device(psi, kappa, interp_down, interp_up, brick_of_cell, pair_first, pair_second):
    struct = jax.ShapeDtypeStruct
    field = struct((LOCAL, GZ, GY, GX), F32)
    place = lax.axis_index("mesh")
    row = brick_of_cell.reshape(1, CELLS)
    first, second = pair_first.reshape(1, LOCAL), pair_second.reshape(1, LOCAL)
    out = call(
        pack_kernel,
        struct((LANES, LOCAL * BOUND + NUMBERS, NODES_E), BF16),
        [SMEM] + [VMEM] * 5,
        (place.astype(I32).reshape(1), first, second, row, interp_down.T, psi),
    )
    arrived = lax.all_to_all(out, "mesh", 0, 0, tiled=True)
    half = pltpu.VMEM((LOCAL, CELLS // 2, NODES_E), F32)
    edges, up, down, number = call(
        edges_kernel,
        (
            struct((LOCAL, 4, GY, GX), F32),
            struct(((LOCAL * 2 + 1) * GY, GX), F32),
            struct((LOCAL * GY, GX), F32),
            struct((1, SLOTS), I32),
        ),
        [VMEM, VMEM],
        (arrived, kappa),
        [half],
    )
    down = lax.ppermute(down, "mesh", [((i + 1) % LANES, i) for i in range(LANES)])
    up = lax.ppermute(up, "mesh", [(i, (i + 1) % LANES) for i in range(LANES)])
    not_first, not_last = (
        inside.astype(I32).reshape(1) for inside in (place > 0, place < LANES - 1)
    )
    pick, spread, orbitals, upward, u, w, part = call(
        inner_kernel,
        (
            struct((CELLS, SLOTS), BF16),
            struct((SLOTS, CELLS), BF16),
            struct((META, WIDE), BF16),
            struct((NODES_W, NODES_E), BF16),
            field,
            field,
            struct((16, 128), F32),
        ),
        [VMEM] * 8,
        (first, second, row, number, interp_up, arrived, edges, kappa),
        [half],
    )
    ends, sums = call(
        outer_kernel,
        (struct((LOCAL, 2, GY, GX), F32), struct((LANES, 128), F32)),
        [SMEM] * 2 + [VMEM] * 6,
        (not_first, not_last, u, w, part, up, down, kappa),
    )
    sums = lax.all_to_all(sums, "mesh", 0, 0, tiled=True)
    potential, back = call(
        finish_kernel,
        (field, struct((SLOTS, WIDE), BF16)),
        [VMEM, VMEM, VMEM, VMEM, VMEM],
        (sums, u, w, ends, spread),
        [pltpu.VMEM((LOCAL, CELLS, NODES_E), F32)],
    )
    returned = lax.all_to_all(back, "mesh", 0, 0, tiled=True)
    value = call(
        cells_kernel,
        struct((CELLS + META, WIDE), BF16),
        [VMEM] * 3,
        (pick, returned, orbitals),
    )

    def along_x(value, by):
        return lax.ppermute(value, "pair", [(i, (i + by) % ORB) for i in range(ORB)])

    right, left, across = (along_x(value, by) for by in (2, -2, 4))
    me = lax.axis_index("pair").astype(I32)
    mine, others = me.reshape(1), (me ^ 1).reshape(1)
    parts = ()
    for block in (value, across, left):
        parts = add_terms(block, (mine, others), upward, psi, parts)
    own, other = parts
    (other,) = add_terms(right, (others,), upward, psi, (other,))
    given = lax.ppermute(other, "pair", [(i, i ^ 1) for i in range(ORB)])
    (own,) = add_terms(right, (mine,), upward, psi, (own,))
    action = call(
        join_kernel, struct((NODES_W, 1, CELLS), F32), [VMEM, VMEM], (own, given)
    )
    return potential, action.reshape(1, NODES_W, CELLS)


def solution(mesh):
    return jax.shard_map(
        on_device,
        mesh=mesh,
        in_specs=(
            P(None, None, "mesh"),
            P("mesh", None, None),
            P(),
            P(),
            P("mesh"),
            P("pair"),
            P("pair"),
        ),
        out_specs=(P("pair", "mesh", None, None), P("pair", None, "mesh")),
        check_vma=False,
    )
```

```python
import functools
import math

import jax
import jax.numpy as jnp
from jax import lax
from jax.experimental import pallas as pl
from jax.experimental.pallas import tpu as pltpu
from jax.sharding import PartitionSpec as P

F32 = jnp.float32
BF16 = jnp.bfloat16
I32 = jnp.int32
FOUR_PI = 4.0 * math.pi

LANES = 32
BOUND = 16
CELLS = 256
SLOTS = LANES * BOUND
NODES_W = 343
NODES_E = 128
LOCAL = 4
ORB = 8
GZ, GY, GX = 8, 32, 128
WIDE = LOCAL * NODES_E
NUMBERS = 8
META = 8

VMEM = pl.BlockSpec(memory_space=pltpu.VMEM)
SMEM = pl.BlockSpec(memory_space=pltpu.SMEM)
PARAMS = pltpu.CompilerParams(vmem_limit_bytes=16 * 1024 * 1024)


def iota(shape, dim):
    return lax.broadcasted_iota(I32, shape, dim)


def onehot(condition):
    return jnp.where(condition, 1.0, 0.0).astype(BF16)


def dot(left, right):
    return lax.dot_general(left, right, (((1,), (0,)), ((), ())), preferred_element_type=F32)


def dot_nt(left, right):
    return lax.dot_general(left, right, (((1,), (1,)), ((), ())), preferred_element_type=F32)


def dot_tn(left, right):
    return lax.dot_general(left, right, (((0,), (0,)), ((), ())), preferred_element_type=F32)


def call(body, out, specs, args, scratch=(), flops=10**7):
    return pl.pallas_call(
        body,
        out_shape=out,
        in_specs=specs,
        out_specs=jax.tree.map(lambda _: VMEM, out),
        scratch_shapes=list(scratch),
        compiler_params=PARAMS,
        cost_estimate=pl.CostEstimate(flops=flops, bytes_accessed=2**21, transcendentals=0),
    )(*args)


def swap_groups(tiles):
    group = iota((8, 128), 1) >> 4
    for bit in (1, 2, 4):
        low = (group & bit) == 0
        mixed = list(tiles)
        for i in range(8):
            if i & bit == 0:
                j = i | bit
                mixed[i] = jnp.where(low, tiles[i], pltpu.roll(tiles[j], 16 * bit, 1))
                mixed[j] = jnp.where(low, pltpu.roll(tiles[i], 128 - 16 * bit, 1), tiles[j])
        tiles = mixed
    return tiles


def plane_of(kappa, z):
    return jnp.concatenate([kappa[z, pl.ds(c, 8, stride=4), :] for c in range(4)], axis=0)


def beside_xy(plane):
    row, lane = iota((8, 128), 0), iota((GY, 128), 1)
    first, last = plane[0:8], plane[24:32]
    above = jnp.where(row < 7, pltpu.roll(first, 7, 0), 0.0)
    below = jnp.where(row > 0, pltpu.roll(last, 1, 0), 0.0)
    along_y = jnp.concatenate([plane[8:32], above], axis=0) + jnp.concatenate(
        [below, plane[0:24]], axis=0
    )
    right = jnp.where(lane < 127, pltpu.roll(plane, 127, 1), 0.0)
    left = jnp.where(lane > 0, pltpu.roll(plane, 1, 1), 0.0)
    return along_y + right + left


def positions(row):
    target = row >> 8
    member = iota((LANES, CELLS), 0) == target
    order = onehot(iota((CELLS, CELLS), 0) < iota((CELLS, CELLS), 1))
    rank = jnp.where(member, dot(onehot(member), order), 0.0)
    return target, member, jnp.sum(rank, axis=0, keepdims=True).astype(I32)


def slots_of(row):
    target, _, rank = positions(row)
    return iota((SLOTS, CELLS), 0) == target * BOUND + rank


def each(orbitals):
    lane = iota((1, LOCAL), 1)
    return [jnp.max(jnp.where(lane == p, orbitals[...], 0)) for p in range(LOCAL)]


def pack_kernel(here, first, second, row, down, psi, out):
    target, member, rank = positions(row[...])
    sel = onehot(iota((SLOTS, CELLS), 0) == target * BOUND + rank)
    dens = [
        (psi[a].astype(F32) * psi[b].astype(F32)).astype(BF16)
        for a, b in zip(each(first), each(second))
    ]
    rho = dot_tn(down[...], jnp.concatenate(dens, axis=1)).astype(BF16)
    rho = jnp.concatenate([rho[:, p * CELLS : (p + 1) * CELLS] for p in range(LOCAL)], axis=0)
    sent = dot_nt(sel, rho).astype(BF16)
    for p in range(LOCAL):
        part = sent[:, p * NODES_E : (p + 1) * NODES_E]
        out[:, p * BOUND : (p + 1) * BOUND] = part.reshape(LANES, BOUND, NODES_E)
    number = jnp.where(member, (row[...] & 255) + 1, 0).astype(F32).astype(BF16)
    lanes = onehot(iota((NODES_E, CELLS), 0) == rank + BOUND * (here[0] & (NUMBERS - 1)))
    number = jnp.broadcast_to(dot_nt(number, lanes)[:, None], (LANES, NUMBERS, NODES_E))
    out[:, LOCAL * BOUND :] = number.astype(BF16)


def placed_bricks(number, arrived, start, count, skip):
    brick = iota((count, SLOTS), 0)
    brick = brick + start + jnp.where(brick >= count // 2, skip, 0)
    parts = [
        arrived[:, p * BOUND : (p + 1) * BOUND].reshape(SLOTS, NODES_E) for p in range(LOCAL)
    ]
    return dot(onehot(brick == number), jnp.concatenate(parts, axis=1))


def two_layers(placed, p, row, diag):
    tiles = swap_groups([placed[p, pl.ds(row + bx, 8, stride=8), :] for bx in range(8)])
    return [
        FOUR_PI * jnp.concatenate(tiles[4 * a : 4 * a + 4], axis=0) / diag[a] for a in range(2)
    ]


def edges_kernel(arrived, kappa, u_out, up_out, down_out, number_out, placed):
    rows = arrived[:, LOCAL * BOUND :].astype(F32).reshape(4, LANES // 4 * NUMBERS, NODES_E)
    rows = jnp.sum(rows, axis=1, keepdims=True) * (1.0 / NUMBERS)
    number = jnp.concatenate([rows[i] for i in range(4)], axis=1).astype(I32) - 1
    number_out[...] = number
    wide = placed_bricks(number, arrived, 0, 128, 128)
    for p in range(LOCAL):
        placed[p] = wide[:, p * NODES_E : (p + 1) * NODES_E]
    diag = [6.0 + plane_of(kappa, z) for z in (0, 1, GZ - 2, GZ - 1)]
    for p in range(LOCAL):
        u = two_layers(placed, p, 0, diag[:2]) + two_layers(placed, p, 64, diag[2:])
        for i, plane in enumerate(u):
            u_out[p, i] = plane
        for a in range(2):
            up_out[(p * 2 + a) * GY : (p * 2 + a + 1) * GY] = u[2 + a]
        down_out[p * GY : (p + 1) * GY] = u[0]
    up_out[LOCAL * 2 * GY :] = plane_of(kappa, GZ - 1)


def inner_kernel(first, second, row, number, up, arrived, edges, kappa, pick, spread, orbitals, up_out, u_ref, w_out, sums_out, placed):
    pick[...] = jnp.where(slots_of(row[...]), 1.0, 0.0).T.astype(BF16)
    sel = iota((CELLS, SLOTS), 0) == number[...]
    spread[...] = jnp.where(sel, 1.0, 0.0).T.astype(BF16)
    up_out[...] = up[...]
    lane = iota((META, WIDE), 1)
    numbers = jnp.zeros((META, WIDE), I32)
    for p, (a, b) in enumerate(zip(each(first), each(second))):
        numbers = jnp.where(lane == 2 * p, a, jnp.where(lane == 2 * p + 1, b, numbers))
    orbitals[...] = numbers.astype(F32).astype(BF16)
    diag = [6.0 + plane_of(kappa, z) for z in range(GZ)]
    inverse = [1.0 / d for d in diag]
    wide = placed_bricks(number[...], arrived, 64, 128, 0)
    for p in range(LOCAL):
        placed[p] = wide[:, p * NODES_E : (p + 1) * NODES_E]
    rows = []
    for p in range(LOCAL):
        u = [edges[p, 0], edges[p, 1]]
        u += two_layers(placed, p, 0, diag[2:4]) + two_layers(placed, p, 64, diag[4:6])
        u += [edges[p, 2], edges[p, 3]]
        gamma = delta = eps = cross = jnp.zeros((GY, 128), F32)
        before = jnp.zeros((GY, 128), F32)
        for z in range(GZ):
            centre = u[z]
            u_ref[p, z] = centre
            scaled = diag[z] * centre
            gamma += scaled * centre
            image = scaled - beside_xy(centre)
            if z > 0:
                image = image - u[z - 1]
            if z < GZ - 1:
                image = image - u[z + 1]
            if z in (0, GZ - 1):
                w_out[p, z] = image
                continue
            w = image * inverse[z]
            w_out[p, z] = w
            delta += centre * image
            eps += image * w
            cross += w * (beside_xy(w) + 2.0 * before)
            before = w
        rows += [jnp.sum(v, axis=0, keepdims=True) for v in (gamma, delta, eps, eps - cross)]
    sums_out[...] = jnp.concatenate(rows, axis=0)


def outer_kernel(not_first, not_last, u_ref, w_ref, part, up, down, kappa, ends, sums_out):
    keep, keep_high = not_first[0].astype(F32), not_last[0].astype(F32)
    inverse = [1.0 / (6.0 + k) for k in (up[LOCAL * 2 * GY :], plane_of(kappa, 0), plane_of(kappa, GZ - 1))]
    rows = []
    for p in range(LOCAL):
        far, near = (up[(p * 2 + a) * GY : (p * 2 + a + 1) * GY] for a in range(2))
        low, high = u_ref[p, 0], u_ref[p, GZ - 1]
        w_before = keep * (near - (far + low + beside_xy(near)) * inverse[0])
        q_low = w_ref[p, 0] - keep * near
        q_high = w_ref[p, GZ - 1] - keep_high * down[p * GY : (p + 1) * GY]
        w_low, w_high = q_low * inverse[1], q_high * inverse[2]
        ends[p, 0] = w_low
        ends[p, 1] = w_high
        delta = low * q_low + high * q_high
        eps = q_low * w_low + q_high * w_high
        cross = w_low * (beside_xy(w_low) + 2.0 * (w_before + w_ref[p, 1]))
        cross += w_high * (beside_xy(w_high) + 2.0 * w_ref[p, GZ - 2])
        rows += [jnp.zeros((1, 128), F32)]
        rows += [jnp.sum(v, axis=0, keepdims=True) for v in (delta, eps, eps - cross)]
    sums = jnp.sum(jnp.concatenate(rows, axis=0) + part[...], axis=1, keepdims=True)
    spread = jnp.where(iota((16, 128), 1) == iota((16, 128), 0), sums, 0.0)
    sums_out[...] = jnp.broadcast_to(jnp.sum(spread, axis=0, keepdims=True), (LANES, 128))


def finish_kernel(sums, u_ref, w_ref, ends, spread, potential, out, bricks):
    total = jnp.sum(sums[...], axis=0, keepdims=True)
    lane = iota((1, 128), 1)
    for p in range(LOCAL):
        gamma, delta, eps, zeta = (
            jnp.sum(jnp.where(lane == 4 * p + k, total, 0.0), axis=1, keepdims=True) for k in range(4)
        )
        alpha = gamma / delta
        fresh = alpha * alpha * eps - gamma
        grow = 1.0 + fresh / gamma
        energy = grow * grow * delta - 2.0 * grow * alpha * eps + alpha * alpha * zeta
        later = fresh / energy
        on_u = jnp.broadcast_to(alpha + later * grow, (GY, 128))
        on_w = jnp.broadcast_to(later * alpha, (GY, 128))
        for bz in range(4):
            tiles = []
            for a in range(2):
                z = 2 * bz + a
                w = ends[p, z // (GZ - 1)] if z in (0, GZ - 1) else w_ref[p, z]
                x = on_u * u_ref[p, z] - on_w * w
                for c in range(4):
                    tile = x[8 * c : 8 * c + 8]
                    potential[p, z, pl.ds(c, 8, stride=4), :] = tile
                    tiles.append(tile)
            for bx, tile in enumerate(swap_groups(tiles)):
                bricks[p, pl.ds(bz * 64 + bx, 8, stride=8), :] = tile
    wide = jnp.concatenate([bricks[p].astype(BF16) for p in range(LOCAL)], axis=1)
    out[...] = dot(spread[...], wide).astype(BF16)


def cells_kernel(pick, returned, orbitals, out):
    out[:CELLS] = dot(pick[...], returned[...]).astype(BF16)
    out[CELLS:] = orbitals[...]


def terms_kernel(count, started, *refs):
    wanted, (up, psi, block, *totals) = refs[:count], refs[count:]
    if started:
        earlier, totals = totals[:count], totals[count:]
    orbitals = block[CELLS:, :128].astype(F32).astype(I32)
    lane = iota((META, 128), 1)
    read = [jnp.max(jnp.where(lane == k, orbitals, 0)) for k in range(2 * LOCAL)]
    for k, total in enumerate(totals):
        total[...] = earlier[k][...] if started else jnp.zeros_like(total)
    for p in range(LOCAL):
        for k, total in enumerate(totals):

            @pl.when(read[2 * p] == wanted[k][0])
            def _():
                orbital = psi[read[2 * p + 1]].astype(F32)
                cellv = block[:CELLS, p * 128 : (p + 1) * 128]
                total[...] += dot_nt(up[...], cellv) * orbital


def add_terms(block, wanted, up, psi, earlier):
    total = jax.ShapeDtypeStruct((NODES_W, CELLS), F32)
    count = len(wanted)
    return call(
        functools.partial(terms_kernel, count, bool(earlier)),
        (total,) * count,
        [SMEM] * count + [VMEM] * (3 + len(earlier)),
        (*wanted, up, psi, block, *earlier),
    )


def join_kernel(own, given, out):
    out[:, 0, :] = own[...] + given[...]


def on_device(psi, kappa, interp_down, interp_up, brick_of_cell, pair_first, pair_second):
    struct = jax.ShapeDtypeStruct
    field = struct((LOCAL, GZ, GY, GX), F32)
    place = lax.axis_index("mesh")
    row = brick_of_cell.reshape(1, CELLS)
    first, second = pair_first.reshape(1, LOCAL), pair_second.reshape(1, LOCAL)
    out = call(
        pack_kernel,
        struct((LANES, LOCAL * BOUND + NUMBERS, NODES_E), BF16),
        [SMEM] + [VMEM] * 5,
        (place.astype(I32).reshape(1), first, second, row, interp_down.T, psi),
    )
    arrived = lax.all_to_all(out, "mesh", 0, 0, tiled=True)
    half = pltpu.VMEM((LOCAL, CELLS // 2, NODES_E), F32)
    edges, up, down, number = call(
        edges_kernel,
        (
            struct((LOCAL, 4, GY, GX), F32),
            struct(((LOCAL * 2 + 1) * GY, GX), F32),
            struct((LOCAL * GY, GX), F32),
            struct((1, SLOTS), I32),
        ),
        [VMEM, VMEM],
        (arrived, kappa),
        [half],
    )
    down = lax.ppermute(down, "mesh", [((i + 1) % LANES, i) for i in range(LANES)])
    up = lax.ppermute(up, "mesh", [(i, (i + 1) % LANES) for i in range(LANES)])
    not_first, not_last = (
        inside.astype(I32).reshape(1) for inside in (place > 0, place < LANES - 1)
    )
    pick, spread, orbitals, upward, u, w, part = call(
        inner_kernel,
        (
            struct((CELLS, SLOTS), BF16),
            struct((SLOTS, CELLS), BF16),
            struct((META, WIDE), BF16),
            struct((NODES_W, NODES_E), BF16),
            field,
            field,
            struct((16, 128), F32),
        ),
        [VMEM] * 8,
        (first, second, row, number, interp_up, arrived, edges, kappa),
        [half],
    )
    ends, sums = call(
        outer_kernel,
        (struct((LOCAL, 2, GY, GX), F32), struct((LANES, 128), F32)),
        [SMEM] * 2 + [VMEM] * 6,
        (not_first, not_last, u, w, part, up, down, kappa),
    )
    sums = lax.all_to_all(sums, "mesh", 0, 0, tiled=True)
    potential, back = call(
        finish_kernel,
        (field, struct((SLOTS, WIDE), BF16)),
        [VMEM, VMEM, VMEM, VMEM, VMEM],
        (sums, u, w, ends, spread),
        [pltpu.VMEM((LOCAL, CELLS, NODES_E), F32)],
    )
    returned = lax.all_to_all(back, "mesh", 0, 0, tiled=True)
    value = call(
        cells_kernel,
        struct((CELLS + META, WIDE), BF16),
        [VMEM] * 3,
        (pick, returned, orbitals),
    )

    def along_x(value, by):
        return lax.ppermute(value, "pair", [(i, (i + by) % ORB) for i in range(ORB)])

    right, left, across = (along_x(value, by) for by in (2, -2, 4))
    me = lax.axis_index("pair").astype(I32)
    mine, others = me.reshape(1), (me ^ 1).reshape(1)
    parts = ()
    for block in (value, across, right):
        parts = add_terms(block, (mine, others), upward, psi, parts)
    own, other = parts
    (other,) = add_terms(left, (others,), upward, psi, (other,))
    given = lax.ppermute(other, "pair", [(i, i ^ 1) for i in range(ORB)])
    (own,) = add_terms(left, (mine,), upward, psi, (own,))
    action = call(
        join_kernel, struct((NODES_W, 1, CELLS), F32), [VMEM, VMEM], (own, given)
    )
    return potential, action.reshape(1, NODES_W, CELLS)


def solution(mesh):
    return jax.shard_map(
        on_device,
        mesh=mesh,
        in_specs=(
            P(None, None, "mesh"),
            P("mesh", None, None),
            P(),
            P(),
            P("mesh"),
            P("pair"),
            P("pair"),
        ),
        out_specs=(P("pair", "mesh", None, None), P("pair", None, "mesh")),
        check_vma=False,
    )
```
